32 devices in a mesh: narrow: 4 (over y, core), wide: 8 (over z, x).
Axes of the slice: x: 2, y: 2, z: 4, core: 2. Of those that a mesh axis runs over, the one named last changes fastest.
Arguments:
- tokens: bfloat16 [4, 2048, 2048], P('narrow', 'wide'), may hold values from -12 to 12
- cotangent: bfloat16 [4, 2048, 2048], P('narrow', 'wide'), may hold values from -6 to 6
- qkv_weight: bfloat16 [2048, 6144], P('wide'), may hold values from -0.25 to 0.25
- out_weight: bfloat16 [2048, 2048], P('wide'), may hold values from -0.5 to 0.5
- gain_attn: bfloat16 [2048], P('wide'), may hold values from 0.5 to 1.5
- gate_up_weight: bfloat16 [2048, 16384], P('wide'), may hold values from -0.125 to 0.125
- down_weight: bfloat16 [2048, 8192], P('wide'), may hold values from -0.125 to 0.125
- gain_mlp: bfloat16 [2048], P('wide'), may hold values from 0.5 to 1.5
- gate_logit: float32 [16], replicated, may hold values from -2 to 2
- memory_in: float32 [4, 16, 128, 128], P('narrow'), may hold values from -24 to 24
- normalizer_in: float32 [4, 16, 128], P('narrow'), may hold values from 0.25 to 2
Outputs:
- output: bfloat16 [4, 2048, 2048], P('narrow', 'wide')
- grad_tokens: bfloat16 [4, 2048, 2048], P('narrow', 'wide')
- grad_memory_in: float32 [4, 16, 128, 128], P('narrow')
- grad_normalizer_in: float32 [4, 16, 128], P('narrow')
- grad_qkv_weight: float32 [2048, 6144], P('wide')
- grad_out_weight: float32 [2048, 2048], P('wide')
- grad_gain_attn: float32 [2048], P('wide')
- grad_gate_up_weight: float32 [2048, 16384], P('wide')
- grad_down_weight: float32 [2048, 8192], P('wide')
- grad_gain_mlp: float32 [2048], P('wide')
- grad_gate_logit: float32 [16], replicated
The draws below stay inside these ranges and needn't reach their ends.
All inputs are finite; a program needn't handle non-finite values.
Results may differ from the reference program's by a relative error of at most 0.02.
Values may be sent and summed in bfloat16 or wider, within the bound.
No kernel may reach another device: no remote copies, remote signals or barrier semaphores. Data moves between devices by JAX's collectives and lax.ppermute only.
A program may use at most 512 MiB of HBM per device.

```python
import math
import jax
import jax.numpy as jnp
from jax import lax

D = 2048
H = 16
DK = 128
FF = 8192
SEG = 1024
SEQS = 4
LEN = 2048


def draw_tokens(key, part):
    key_common, key_noise, key_rows, key_cols = jax.random.split(key, 4)
    common = jax.random.normal(key_common, (SEQS, 1, D), jnp.float32)
    noise = jax.random.normal(key_noise, (SEQS, LEN, D), jnp.float32)
    row_scale = jnp.exp(jax.random.uniform(key_rows, (SEQS, LEN, 1), jnp.float32, -1.2, 1.1))
    col_scale = jnp.exp(jax.random.uniform(key_cols, (1, 1, D), jnp.float32, -0.7, 0.7))
    mixed = (0.8 * common + 0.6 * noise) * row_scale * col_scale
    return jnp.clip(mixed, -12.0, 12.0).astype(jnp.bfloat16)


def level_of(rng, extent, shards, low, high):
    def one(axis_at, blocks):
        heights = jax.random.uniform(jax.random.fold_in(jax.random.fold_in(rng, 6), axis_at), (blocks,), jnp.float32, low / len(shards), high / len(shards))
        return jnp.repeat(jnp.exp(heights), extent[axis_at] // blocks).reshape((-1,) + (1,) * (len(extent) - axis_at - 1))

    level = one(*shards[0])
    for cut in shards[1:]:
        level = level * one(*cut)
    return level


def scatter_about(stream_key, dims, deviation, limit, cuts=(), dtype=jnp.bfloat16):
    loudness = level_of(stream_key, dims, cuts, -0.22, 0.18) if cuts else 1.0
    array = jax.random.normal(stream_key, dims, jnp.float32) * deviation * loudness
    return jnp.minimum(jnp.maximum(array, -limit), limit).astype(dtype)


def setup_inputs(seed: int = 0) -> dict:
    key_list = jax.random.split(jax.random.key(seed), 12)
    tokens = draw_tokens(jax.random.fold_in(key_list[11], 71), 0)
    cotangent = scatter_about(key_list[1], (SEQS, LEN, D), 1.0, 6.0, ((0, 4), (1, 8)))
    qkv_weight = scatter_about(key_list[2], (D, 3 * D), (D // 4) ** -0.5, 0.25, ((0, 8),))
    out_weight = scatter_about(key_list[3], (D, D), (D // 16) ** -0.5, 0.5, ((0, 8),))
    gain_attn = jnp.clip(1.0 + 0.1 * jax.random.normal(key_list[4], (D,), jnp.float32), 0.5, 1.5).astype(jnp.bfloat16)
    gate_up_weight = scatter_about(key_list[5], (D, 2 * FF), D ** -0.5, 0.125, ((0, 8),))
    down_weight = scatter_about(key_list[6], (D, FF), (FF // 4) ** -0.5, 0.125, ((0, 8),))
    gain_mlp = jnp.clip(1.0 + 0.1 * jax.random.normal(key_list[7], (D,), jnp.float32), 0.5, 1.5).astype(jnp.bfloat16)
    gate_logit = jnp.clip(jax.random.uniform(key_list[8], (H,), jnp.float32, -2.0, 2.0), -2.0, 2.0)
    memory_in = scatter_about(key_list[9], (SEQS, H, DK, DK), 4.0, 24.0, ((0, 4),), jnp.float32)
    normalizer_in = jnp.clip(jnp.exp(math.log(2.0) - 2.0794415 * jax.random.uniform(key_list[10], (SEQS, H, DK), jnp.float32) ** level_of(key_list[10], (SEQS, H, DK), ((0, 4),), -0.2, 0.2)), 0.25, 2.0)
    return dict(tokens=tokens, cotangent=cotangent, qkv_weight=qkv_weight, out_weight=out_weight, gain_attn=gain_attn, gate_up_weight=gate_up_weight, down_weight=down_weight, gain_mlp=gain_mlp, gate_logit=gate_logit, memory_in=memory_in, normalizer_in=normalizer_in)


@jax.custom_vjp
def low(v):
    return lax.optimization_barrier(v.astype(jnp.bfloat16)).astype(jnp.float32)

@jax.custom_vjp
def low_back(v):
    return v

def low_keep(v):
    return (low(v), None)

def low_pass(kept, grad):
    return (grad,)

def back_keep(v):
    return (v, None)

def back_low(kept, grad):
    return (low(grad),)
low.defvjp(low_keep, low_pass)
low_back.defvjp(back_keep, back_low)
EPSILON = 1e-06

def hdot(left, right):
    return jnp.dot(left, right, precision=lax.Precision.HIGHEST, preferred_element_type=jnp.float32)

def hsum(form, left, right):
    return jnp.einsum(form, left, right, precision=lax.Precision.HIGHEST, preferred_element_type=jnp.float32)

def segment_attention(parts):
    queries, keys, values = parts
    scores = low_back(hsum('thd,shd->hts', queries, keys) * DK ** (-0.5))
    places = jnp.arange(SEG)
    causal = places[None, :] <= places[:, None]
    scores = jnp.where(causal[None], scores, -1e+30)
    highest = lax.optimization_barrier(jnp.max(scores, axis=-1, keepdims=True))
    raised = jnp.exp(scores - highest)
    attn_probs = low(raised / lax.optimization_barrier(jnp.sum(raised, axis=-1, keepdims=True)))
    return low_back(hsum('hts,shd->thd', attn_probs, values))

def sequence_forward(x_row, memory, normalizer, weights):
    qkv_w, out_w, gain_one, gate_up_w, down_w, gain_two, logits = weights
    count = LEN // SEG
    scale_one = lax.rsqrt(lax.optimization_barrier(jnp.mean(x_row * x_row, axis=-1, keepdims=True)) + EPSILON)
    normed_one = low(x_row * scale_one * gain_one)
    projected = low(low_back(hdot(normed_one, qkv_w)))
    queries = projected[:, :D].reshape(count, SEG, H, DK)
    keys = projected[:, D:2 * D].reshape(count, SEG, H, DK)
    values = projected[:, 2 * D:].reshape(count, SEG, H, DK)
    direct = lax.map(jax.checkpoint(segment_attention), (queries, keys, values))
    lift_q = jax.nn.elu(queries) + 1.0
    lift_k = jax.nn.elu(keys) + 1.0
    part_mem = hsum('nthd,nthe->nhde', lift_k, values) / SEG
    part_norm = lax.optimization_barrier(jnp.sum(lift_k, axis=1)) / SEG
    prior_mem = jnp.concatenate([jnp.zeros((1, H, DK, DK), jnp.float32), jnp.cumsum(part_mem, axis=0)[:-1]], axis=0)
    prior_norm = jnp.concatenate([jnp.zeros((1, H, DK), jnp.float32), jnp.cumsum(part_norm, axis=0)[:-1]], axis=0)
    read_mem = memory[None] + prior_mem
    read_norm = normalizer[None] + prior_norm
    numerator = hsum('nthd,nhde->nthe', lift_q, read_mem)
    denominator = hsum('nthd,nhd->nth', lift_q, read_norm)
    recalled = low_back(numerator / denominator[..., None])
    mixing = jax.nn.sigmoid(logits)[None, None, :, None]
    attended = low((mixing * recalled + (1.0 - mixing) * direct).reshape(LEN, D))
    middle = x_row + low_back(hdot(attended, out_w))
    scale_two = lax.rsqrt(lax.optimization_barrier(jnp.mean(middle * middle, axis=-1, keepdims=True)) + EPSILON)
    normed_two = low(middle * scale_two * gain_two)
    gate_up = low_back(hdot(normed_two, gate_up_w))
    activation = low(jax.nn.silu(gate_up[:, :FF]) * gate_up[:, FF:])
    return middle + low_back(hdot(activation, down_w.T))

def reference(tokens, cotangent, qkv_weight, out_weight, gain_attn, gate_up_weight, down_weight, gain_mlp, gate_logit, memory_in, normalizer_in):
    weights = (qkv_weight.astype(jnp.float32), out_weight.astype(jnp.float32), gain_attn.astype(jnp.float32), gate_up_weight.astype(jnp.float32), down_weight.astype(jnp.float32), gain_mlp.astype(jnp.float32), gate_logit.astype(jnp.float32))

    def forward(x_all, weight_set, memory_all, normalizer_all):

        def single(parts):
            return jax.checkpoint(sequence_forward)(parts[0], parts[1], parts[2], weight_set)
        return lax.map(single, (x_all, memory_all, normalizer_all))
    result, pull = jax.vjp(forward, tokens.astype(jnp.float32), weights, memory_in, normalizer_in)
    grad_x, grad_w, grad_mem, grad_norm = pull(cotangent.astype(jnp.float32))
    return (result.astype(jnp.bfloat16), grad_x.astype(jnp.bfloat16), grad_mem, grad_norm, grad_w[0], grad_w[1], grad_w[2], grad_w[3], grad_w[4], grad_w[5], grad_w[6])
```

```python
import functools

import jax
import jax.numpy as jnp
from jax import lax
from jax.experimental import pallas as pl
from jax.experimental.pallas import tpu as pltpu
from jax.sharding import PartitionSpec as P

D = 2048
H = 16
DK = 128
FF = 8192
SEG = 1024
EPSILON = 1e-06
F32 = jnp.float32
BF16 = jnp.bfloat16
GROUP = 8


def swap_x(v):
    n = lax.axis_size("wide")
    return lax.ppermute(v, "wide", [(i, i ^ 1) for i in range(n)])


def swap_y(v):
    return lax.ppermute(v, "narrow", [(i, i ^ 2) for i in range(4)])


def swap_core(v):
    return lax.ppermute(v, "narrow", [(i, i ^ 1) for i in range(4)])


def swap_z(v, d):
    n = lax.axis_size("wide")
    return lax.ppermute(v, "wide", [(i, i ^ (2 * d)) for i in range(n)])


def ring_z(v):
    n = lax.axis_size("wide")
    return lax.ppermute(v, "wide", [(i, (i - 2) % n) for i in range(n)])


def offset_bits(r):
    return (r >> 1) & 1, (r >> 2) & 1, r & 1


def absolute(r):
    y, core, x = offset_bits(r)
    return y * 4 + core * 2 + x


def send_offset(v, r):
    y, core, x = offset_bits(r)
    n = lax.axis_size("wide")
    flip = y * 2 + core
    route = [(a * n + b, (a ^ flip) * n + (b ^ x)) for a in range(4) for b in range(n)]
    return lax.ppermute(v, ("narrow", "wide"), route)


def gather_group(v):
    half = v.shape[0] // 2
    a, b = v[:half], v[half:]
    a1 = swap_x(a)
    b2 = swap_y(b)
    a2 = swap_y(jnp.stack([a, a1]))
    b1 = swap_x(jnp.stack([b, b2]))
    own = jnp.concatenate([a, b, a1, b1[0], a2[0], b2, a2[1], b1[1]], axis=0)
    return own, swap_core(own)


def add(a, b):
    return (a.astype(F32) + b.astype(F32)).astype(BF16)


def scatter_group(own, other):
    rows = own.shape[0] // 4
    half = rows // 2
    q = own.astype(F32) + swap_core(other).astype(F32)
    q = q.reshape(4, 2, half, -1)
    qs = q.astype(BF16)
    ay = swap_y(qs[2:4, 0])
    bx = swap_x(jnp.stack([qs[1, 1], qs[3, 1]]))
    a0, a1 = q[0, 0] + ay[0].astype(F32), q[1, 0] + ay[1].astype(F32)
    b0, b2 = q[0, 1] + bx[0].astype(F32), q[2, 1] + bx[1].astype(F32)
    a = a0 + swap_x(a1.astype(BF16)).astype(F32)
    b = b0 + swap_y(b2.astype(BF16)).astype(F32)
    return jnp.concatenate([a, b], axis=0)


def exchange_group(blocks):
    return [blocks[0]] + [send_offset(blocks[r], r) for r in range(1, GROUP)]


def by_bit(pair, bit):
    a, b = pair
    return jnp.where(bit == 0, jnp.stack([a, b]), jnp.stack([b, a]))


def by_index(parts, index):
    if len(parts) == 2:
        return by_bit(parts, index)
    out = jnp.zeros((len(parts),) + parts[0].shape, parts[0].dtype)
    for d, part in enumerate(parts):
        out = lax.dynamic_update_slice_in_dim(out, part[None], index ^ d, 0)
    return out


def gather_rows(weight, starts, width, z, x, n):
    c = n * 2 + x
    mine = jnp.concatenate(
        [lax.dynamic_slice_in_dim(weight, s + c * width, width, 1) for s in starts], axis=1
    )
    theirs = jnp.concatenate(
        [lax.dynamic_slice_in_dim(weight, s + (c ^ 1) * width, width, 1) for s in starts], axis=1
    )
    pair = by_bit([mine, swap_x(theirs)], x)
    rows = pair.shape[0] * pair.shape[1]
    block = pair.reshape(rows, -1)
    count = lax.axis_size("wide") // 2
    out = jnp.zeros((count * rows, block.shape[1]), block.dtype)
    out = lax.dynamic_update_slice_in_dim(out, block, z * rows, 0)
    for k in range(1, count):
        block = ring_z(block)
        out = lax.dynamic_update_slice_in_dim(out, block, lax.rem(z + k, count) * rows, 0)
    return out


def reduce_rows(partial, z):
    count = lax.axis_size("wide") // 2
    rows = partial.shape[0] // count

    def block(k):
        return lax.dynamic_slice_in_dim(partial, lax.rem(z + k, count) * rows, rows, 0)

    running = block(1)
    for k in range(2, count + 1):
        running = ring_z(running).astype(F32) + block(k).astype(F32)
        if k < count:
            running = running.astype(BF16)
    return running


def spread_columns(summed, x):
    rows = summed.shape[0] // 2
    short = summed.astype(BF16)
    keep = lax.dynamic_slice_in_dim(short, x * rows, rows, 0)
    give = lax.dynamic_slice_in_dim(short, (1 - x) * rows, rows, 0)
    pair = jnp.stack([keep, swap_x(give)])
    four = jnp.concatenate([pair, swap_y(pair)], axis=0)
    return four, swap_core(four)


def assemble_kernel(parts, low, high, order, a_ref, b_ref, o_ref):
    del parts, low, high
    which = order[pl.program_id(0)]

    @pl.when(which < 4)
    def _():
        o_ref[...] = a_ref[0].astype(o_ref.dtype)

    @pl.when(which >= 4)
    def _():
        o_ref[...] = b_ref[0].astype(o_ref.dtype)


def assemble(own, other, c, parts, dtype):
    rows = own.shape[1]
    width = own.shape[2] // parts
    flips = c ^ jnp.arange(GROUP, dtype=jnp.int32)
    order = ((flips >> 1) & 1) * 4 + ((flips >> 2) & 1) * 2 + (flips & 1)
    step = min(rows, 256)
    return pl.pallas_call(
        functools.partial(assemble_kernel, parts, 0, 0),
        grid_spec=pltpu.PrefetchScalarGridSpec(
            num_scalar_prefetch=1,
            grid=(GROUP, parts, rows // step),
            in_specs=[
                pl.BlockSpec((1, step, width), lambda j, p, i, o: (jnp.minimum(o[j], 3), i, p)),
                pl.BlockSpec((1, step, width), lambda j, p, i, o: (jnp.maximum(o[j] - 4, 0), i, p)),
            ],
            out_specs=pl.BlockSpec((step, width), lambda j, p, i, o: (i, p * GROUP + j)),
        ),
        out_shape=jax.ShapeDtypeStruct((rows, parts * GROUP * width), dtype),
        compiler_params=pltpu.CompilerParams(vmem_limit_bytes=24 * 2**20),
    )(order, own, other)


def dot(a, b):
    return jnp.dot(a, b, preferred_element_type=F32)


def dot_t(a, b):
    return lax.dot_general(a, b, (((1,), (1,)), ((), ())), preferred_element_type=F32)


def t_dot(a, b):
    return lax.dot_general(a, b, (((0,), (0,)), ((), ())), preferred_element_type=F32)


def norm_back(grad_unit, unit_rows, scale_rows):
    return scale_rows * (
        grad_unit - unit_rows * jnp.mean(grad_unit * unit_rows, axis=-1, keepdims=True)
    )


def elu_slope(inputs):
    return jnp.where(inputs > 0, 1.0, jnp.exp(jnp.minimum(inputs, 0.0)))


def body(
    tokens,
    cotangent,
    qkv_weight,
    out_weight,
    gain_attn,
    gate_up_weight,
    down_weight,
    gain_mlp,
    gate_logit,
    memory_in,
    normalizer_in,
):
    wide = lax.axis_size("wide")
    n = lax.axis_index("narrow")
    w = lax.axis_index("wide")
    z, x = w // 2, w % 2
    c = n * 2 + x
    rows_here = tokens.shape[1]
    shard = qkv_weight.shape[0]
    span = SEG // rows_here
    zspan = span // 2
    zi = z % zspan
    segments = wide // span
    units = GROUP // zspan
    head_cols = D // GROUP
    ff_cols = FF // GROUP
    scale = DK ** (-0.5)

    inputs = tokens[0].astype(F32)
    scale_one = lax.rsqrt(jnp.mean(inputs * inputs, axis=-1, keepdims=True) + EPSILON)
    unit_one = inputs * scale_one
    gains = lax.all_gather(jnp.stack([gain_attn, gain_mlp]), "wide", axis=1, tiled=True)
    gains = gains.astype(F32)
    gain_one, gain_two = gains[0], gains[1]
    normed_one = (unit_one * gain_one).astype(BF16)
    one_own, one_other = gather_group(normed_one)

    qkv_c = gather_rows(qkv_weight, (0, D, 2 * D), head_cols, z, x, n)
    out_quarter = lax.dynamic_slice_in_dim(out_weight, n * (D // 4), D // 4, 1)
    out_all = lax.all_gather(out_quarter, ("narrow", "wide"), axis=0)
    out_full = (
        out_all.reshape(4, wide, shard, D // 4).transpose(1, 2, 0, 3).reshape(D, D)
    )
    gate_c = gather_rows(gate_up_weight, (0,), ff_cols, z, x, n)
    up_c = gather_rows(gate_up_weight, (FF,), ff_cols, z, x, n)
    down_c = gather_rows(down_weight, (0,), ff_cols, z, x, n)

    cot = cotangent[0]
    cot_own, cot_other = gather_group(cot)

    def to_units(flat, parts):
        v = flat.reshape(2, 2, 2, rows_here, parts, 2, DK).transpose(2, 5, 0, 1, 4, 3, 6)
        v = by_bit([v[0], v[1]], x)
        v = v.transpose(1, 2, 3, 4, 0, 5, 6).reshape(GROUP, parts, 2 * rows_here, DK)
        blocks = []
        for d in range(zspan):
            block = lax.dynamic_slice_in_dim(v, (zi ^ d) * units, units, 0)
            blocks.append(block if d == 0 else swap_z(block, d))
        v = by_index(blocks, zi)
        return v.transpose(1, 2, 0, 3, 4).reshape(units, parts, SEG, DK)

    def from_units(v, parts):
        v = v.reshape(units, parts, zspan, 2 * rows_here, DK)
        blocks = []
        for d in range(zspan):
            block = lax.dynamic_slice_in_dim(v, zi ^ d, 1, 2)[:, :, 0]
            blocks.append(block if d == 0 else swap_z(block, d))
        v = by_index(blocks, zi).reshape(2, 2, 2, parts, 2, rows_here, DK)
        v = by_bit([v[:, :, :, :, 0], v[:, :, :, :, 1]], x)
        v = v.transpose(2, 3, 0, 5, 4, 1, 6)
        return v.reshape(GROUP * rows_here, parts * head_cols)

    one_all = jnp.concatenate([one_own, one_other], axis=0)
    projected = dot(one_all, qkv_c).astype(BF16)
    qkv_units = to_units(projected, 3)
    queries, keys, values = qkv_units[:, 0], qkv_units[:, 1], qkv_units[:, 2]

    positions = jnp.arange(SEG)
    allowed = positions[None, :] <= positions[:, None]
    raw = jnp.einsum("utd,usd->uts", queries, keys, preferred_element_type=F32) * scale
    scores = jnp.where(allowed[None], raw, -1e30)
    highest = jnp.max(scores, axis=-1, keepdims=True)
    raised = jnp.exp(scores - highest)
    attn_probs = raised / jnp.sum(raised, axis=-1, keepdims=True)
    short_probs = attn_probs.astype(BF16)
    direct = jnp.einsum("uts,usd->utd", short_probs, values, preferred_element_type=F32)

    head_count = max(1, units // 4)
    seq_count = units // head_count
    first_head = (zi * units) // 4
    first_seq = (zi * units) % 4
    held = jnp.concatenate([memory_in[0], normalizer_in[0][:, None]], axis=1)
    fetched = []
    for offset in range(4):
        core, y = offset >> 1, offset & 1
        flip = y * 2 + core
        block = lax.dynamic_slice_in_dim(
            held, ((n ^ flip) * 2 + x) * 2 + first_head, head_count, 0
        )
        if flip:
            block = lax.ppermute(block, "narrow", [(i, i ^ flip) for i in range(4)])
        fetched.append(block)
    mem_in = jnp.stack(fetched, axis=1)
    mem_in = lax.dynamic_slice_in_dim(mem_in, first_seq, seq_count, 1)
    mem_in = mem_in.reshape(units, DK + 1, DK)

    query_f, key_f, value_f = (a.astype(F32) for a in (queries, keys, values))
    lift_q = jax.nn.elu(query_f) + 1.0
    lift_k = jax.nn.elu(key_f) + 1.0
    part_mem = jnp.einsum("utd,ute->ude", lift_k, value_f, preferred_element_type=F32)
    part_norm = jnp.sum(lift_k, axis=1)
    part = jnp.concatenate([part_mem, part_norm[:, None]], axis=1) / SEG
    read = mem_in
    for k in range(1, segments):
        read = read + lax.ppermute(
            part, "wide", [(i, i + k * span) for i in range(wide - k * span)]
        )
    read_mem, read_norm = read[:, :DK], read[:, DK]
    numerator = jnp.einsum("utd,ude->ute", lift_q, read_mem, preferred_element_type=F32)
    denominator = jnp.sum(lift_q * read_norm[:, None], axis=-1, keepdims=True)
    recalled = numerator / denominator

    unit_heads = c * 2 + (zi * units + jnp.arange(units)) // 4
    mixing = jax.nn.sigmoid(gate_logit[unit_heads])
    mix = mixing[:, None, None]
    attended_units = (mix * recalled + (1.0 - mix) * direct).astype(BF16)
    attended_c = from_units(attended_units[:, None], 1).reshape(GROUP, rows_here, head_cols)
    sent = exchange_group([attended_c[r] for r in range(GROUP)])
    attended = assemble(jnp.stack(sent[:4]), jnp.stack(sent[4:]), c, 1, BF16)

    middle = inputs + dot(attended, out_full)
    scale_two = lax.rsqrt(jnp.mean(middle * middle, axis=-1, keepdims=True) + EPSILON)
    unit_two = middle * scale_two
    normed_two = (unit_two * gain_two).astype(BF16)
    two_own, two_other = gather_group(normed_two)
    two_all = jnp.concatenate([two_own, two_other], axis=0)
    cot_all = jnp.concatenate([cot_own, cot_other], axis=0)

    gate_part = dot(two_all, gate_c)
    up_part = dot(two_all, up_c)
    gate_sig = jax.nn.sigmoid(gate_part)
    activation = (gate_part * gate_sig * up_part).astype(BF16)

    def group_sum(product):
        half = 4 * rows_here
        return scatter_group(product[:half], product[half:])

    output = (middle + group_sum(dot_t(activation, down_c).astype(BF16))).astype(BF16)[None]

    grad_down_c = reduce_rows(t_dot(cot_all, activation).astype(BF16), z)
    grad_activ = dot(cot_all, down_c)
    grad_gate = (grad_activ * up_part * gate_sig * (1.0 + gate_part * (1.0 - gate_sig))).astype(BF16)
    grad_upper = (grad_activ * gate_part * gate_sig).astype(BF16)
    grad_normed_two = group_sum(
        (dot_t(grad_gate, gate_c) + dot_t(grad_upper, up_c)).astype(BF16)
    )
    grad_gate_c = reduce_rows(t_dot(two_all, grad_gate).astype(BF16), z)
    grad_up_c = reduce_rows(t_dot(two_all, grad_upper).astype(BF16), z)
    grad_gain_two = jnp.sum(grad_normed_two * unit_two, axis=0)
    grad_middle = cot.astype(F32) + norm_back(grad_normed_two * gain_two, unit_two, scale_two)

    grad_branch = grad_middle.astype(BF16)
    grad_att_rows = dot_t(grad_branch, out_full).astype(BF16)
    sent = exchange_group(
        [
            lax.dynamic_slice_in_dim(grad_att_rows, (c ^ absolute(r)) * head_cols, head_cols, 1)
            for r in range(GROUP)
        ]
    )
    grad_att = to_units(jnp.concatenate(sent, axis=0), 1)[:, 0].astype(F32)

    unit_logit = jnp.sum(grad_att * (recalled - direct), axis=(1, 2)) * mixing * (1.0 - mixing)
    grad_logit = jnp.sum(
        jnp.where(unit_heads[:, None] == jnp.arange(H)[None], unit_logit[:, None], 0.0), axis=0
    )
    grad_direct = ((1.0 - mix) * grad_att).astype(BF16)
    grad_recall = (mix * grad_att).astype(BF16).astype(F32)
    grad_probs = jnp.einsum("utd,usd->uts", grad_direct, values, preferred_element_type=F32)
    inner = jnp.sum(attn_probs * grad_probs, axis=-1, keepdims=True)
    grad_scores = (attn_probs * (grad_probs - inner)).astype(BF16)
    grad_q_dot = jnp.einsum("uts,usd->utd", grad_scores, keys, preferred_element_type=F32) * scale
    grad_k_dot = jnp.einsum("uts,utd->usd", grad_scores, queries, preferred_element_type=F32) * scale
    grad_v_dot = jnp.einsum("uts,utd->usd", short_probs, grad_direct, preferred_element_type=F32)

    grad_numer = grad_recall / denominator
    grad_denom = -jnp.sum(grad_recall * recalled, axis=-1, keepdims=True) / denominator
    grad_lift_q = (
        jnp.einsum("ute,ude->utd", grad_numer, read_mem, preferred_element_type=F32)
        + grad_denom * read_norm[:, None]
    )
    grad_read_mem = jnp.einsum("utd,ute->ude", lift_q, grad_numer, preferred_element_type=F32)
    grad_read_norm = jnp.sum(grad_denom * lift_q, axis=1)
    grad_read = jnp.concatenate([grad_read_mem, grad_read_norm[:, None]], axis=1)
    later = jnp.zeros_like(grad_read)
    for k in range(1, segments):
        later = later + lax.ppermute(
            grad_read, "wide", [(i + k * span, i) for i in range(wide - k * span)]
        )
    later = later / SEG
    later_mem, later_norm = later[:, :DK], later[:, DK]
    grad_lift_k = (
        jnp.einsum("ute,ude->utd", value_f, later_mem, preferred_element_type=F32)
        + later_norm[:, None]
    )
    grad_v_mem = jnp.einsum("utd,ude->ute", lift_k, later_mem, preferred_element_type=F32)
    grad_units = jnp.stack(
        [
            grad_q_dot + grad_lift_q * elu_slope(query_f),
            grad_k_dot + grad_lift_k * elu_slope(key_f),
            grad_v_dot + grad_v_mem,
        ],
        axis=1,
    ).astype(BF16)
    grad_projected = from_units(grad_units, 3)

    grad_normed_one = group_sum(dot_t(grad_projected, qkv_c).astype(BF16))
    grad_gain_one = jnp.sum(grad_normed_one * unit_one, axis=0)
    grad_tokens = (
        grad_middle + norm_back(grad_normed_one * gain_one, unit_one, scale_one)
    ).astype(BF16)[None]
    grad_qkv_c = reduce_rows(t_dot(one_all, grad_projected).astype(BF16), z)

    att_own, att_other = gather_group(attended)
    att_all = jnp.concatenate([att_own, att_other], axis=0)
    sent = exchange_group(
        [
            lax.dynamic_slice_in_dim(grad_branch, (c ^ absolute(r)) * head_cols, head_cols, 1)
            for r in range(GROUP)
        ]
    )
    grad_out_c = reduce_rows(t_dot(att_all, jnp.concatenate(sent, axis=0)).astype(BF16), z)

    def whole_rows(summed, parts):
        own, other = spread_columns(summed, x)
        return assemble(own, other, c, parts, F32)

    grad_gate_up = whole_rows(jnp.concatenate([grad_gate_c, grad_up_c], axis=1), 2)
    grad_down = whole_rows(grad_down_c, 1)
    grad_qkv = whole_rows(grad_qkv_c, 3)
    grad_out = whole_rows(grad_out_c, 1)

    placed = jnp.zeros((GROUP, DK + 1, DK), BF16)
    placed = lax.dynamic_update_slice_in_dim(placed, grad_read.astype(BF16), zi * units, 0)
    placed = placed.reshape(2, 4, DK + 1, DK)
    got = []
    for flip in range(4):
        core, y = flip & 1, flip >> 1
        block = placed[:, core * 2 + y]
        if flip:
            block = lax.ppermute(block, "narrow", [(i, i ^ flip) for i in range(4)])
        got.append(block)
    by_narrow = by_index(got, n)[:, None]
    heads = jnp.zeros((4, 2, 2, DK + 1, DK), BF16)
    heads = lax.dynamic_update_slice_in_dim(heads, by_narrow, x, 1)
    heads = lax.psum(heads.reshape(H, DK + 1, DK), "wide").astype(F32)

    small = lax.psum(
        jnp.concatenate([grad_gain_one, grad_gain_two, grad_logit]), ("narrow", "wide")
    )
    gain_one_sum = lax.dynamic_slice_in_dim(small, w * shard, shard, 0)
    gain_two_sum = lax.dynamic_slice_in_dim(small, D + w * shard, shard, 0)
    return (
        output,
        grad_tokens,
        heads[None, :, :DK],
        heads[None, :, DK],
        grad_qkv,
        grad_out,
        gain_one_sum,
        grad_gate_up,
        grad_down,
        gain_two_sum,
        small[2 * D :],
    )


def solution(mesh):
    return jax.shard_map(
        body,
        mesh=mesh,
        in_specs=(
            P("narrow", "wide", None),
            P("narrow", "wide", None),
            P("wide", None),
            P("wide", None),
            P("wide"),
            P("wide", None),
            P("wide", None),
            P("wide"),
            P(),
            P("narrow", None, None, None),
            P("narrow", None, None),
        ),
        out_specs=(
            P("narrow", "wide", None),
            P("narrow", "wide", None),
            P("narrow", None, None, None),
            P("narrow", None, None),
            P("wide", None),
            P("wide", None),
            P("wide"),
            P("wide", None),
            P("wide", None),
            P("wide"),
            P(),
        ),
        check_vma=False,
    )
```

```python
import functools

import jax
import jax.numpy as jnp
from jax import lax
from jax.experimental import pallas as pl
from jax.experimental.pallas import tpu as pltpu
from jax.sharding import PartitionSpec as P

D = 2048
H = 16
DK = 128
FF = 8192
SEG = 1024
EPSILON = 1e-06
F32 = jnp.float32
BF16 = jnp.bfloat16
GROUP = 8


def swap_x(v):
    n = lax.axis_size("wide")
    return lax.ppermute(v, "wide", [(i, i ^ 1) for i in range(n)])


def swap_y(v):
    return lax.ppermute(v, "narrow", [(i, i ^ 2) for i in range(4)])


def swap_core(v):
    return lax.ppermute(v, "narrow", [(i, i ^ 1) for i in range(4)])


def swap_z(v, d):
    n = lax.axis_size("wide")
    return lax.ppermute(v, "wide", [(i, i ^ (2 * d)) for i in range(n)])


def offset_bits(r):
    return (r >> 1) & 1, (r >> 2) & 1, r & 1


def absolute(r):
    y, core, x = offset_bits(r)
    return y * 4 + core * 2 + x


def send_offset(v, r):
    y, core, x = offset_bits(r)
    n = lax.axis_size("wide")
    flip = y * 2 + core
    route = [(a * n + b, (a ^ flip) * n + (b ^ x)) for a in range(4) for b in range(n)]
    return lax.ppermute(v, ("narrow", "wide"), route)


def plane(v):
    return [v] + [send_offset(v, r) for r in range(1, 4)]


def both_cores(pieces):
    return pieces + [swap_core(p) for p in pieces]


def scatter_start(partial):
    rows = partial.shape[0] // GROUP
    parts = [partial[r * rows : (r + 1) * rows] for r in range(GROUP)]
    sums = [None] * 4
    for r in (3, 1, 2, 0):
        sums[r] = parts[r].astype(F32) + swap_core(parts[4 + r]).astype(F32)
    return [sums[0]] + [v.astype(BF16) for v in sums[1:]]


def scatter_sends(sums):
    return [sums[0]] + [send_offset(sums[r], r) for r in range(1, 4)]


def scatter_total(got):
    return got[0] + got[1].astype(F32) + got[2].astype(F32) + got[3].astype(F32)


def join_kernel(*refs):
    out = refs[-1]
    rows = refs[0].shape[0]
    for i, piece in enumerate(refs[:-1]):
        out[i * rows : (i + 1) * rows] = piece[...]


def join(pieces):
    rows, columns = pieces[0].shape
    step = min(columns, 512)
    return pl.pallas_call(
        join_kernel,
        grid=(columns // step,),
        in_specs=[pl.BlockSpec((rows, step), lambda j: (0, j))] * len(pieces),
        out_specs=pl.BlockSpec((len(pieces) * rows, step), lambda j: (0, j)),
        out_shape=jax.ShapeDtypeStruct((len(pieces) * rows, columns), pieces[0].dtype),
        compiler_params=pltpu.CompilerParams(vmem_limit_bytes=24 * 2**20),
    )(*pieces)


def exchange_group(blocks):
    return [blocks[0]] + [send_offset(blocks[r], r) for r in range(1, GROUP)]


def by_bit(pair, bit):
    a, b = pair
    return jnp.where(bit == 0, jnp.stack([a, b]), jnp.stack([b, a]))


def by_index(parts, index):
    if len(parts) == 2:
        return by_bit(parts, index)
    out = jnp.zeros((len(parts),) + parts[0].shape, parts[0].dtype)
    for d, part in enumerate(parts):
        out = lax.dynamic_update_slice_in_dim(out, part[None], index ^ d, 0)
    return out


def after(v, *others):
    return lax.optimization_barrier((v, others))[0]


def z_lines():
    n = lax.axis_size("wide")
    return [list(range(x, n, 2)) for x in range(2)]


def eighth_block(parts, x, n):
    c = n * 2 + x

    def columns(eighth):
        return jnp.concatenate(
            [lax.dynamic_slice_in_dim(a, s + eighth * m, m, 1) for a, s, m in parts], axis=1
        )

    give = columns(c ^ 1)
    pair = by_bit([columns(c), swap_x(give)], x)
    return pair.reshape(pair.shape[0] * pair.shape[1], -1), give


def gather_rows(block):
    return lax.all_gather(block, "wide", axis=0, tiled=True, axis_index_groups=z_lines())


def reduce_rows(partial):
    return lax.psum_scatter(
        partial, "wide", scatter_dimension=0, tiled=True, axis_index_groups=z_lines()
    )


def gather_gains(v, w):
    n = lax.axis_size("wide")
    blocks = [v]
    for d in range(1, n):
        blocks.append(lax.ppermute(v, "wide", [(i, i ^ d) for i in range(n)]))
    return by_index(blocks, w).transpose(1, 0, 2).reshape(2, -1)


def sum_z(v):
    d = 1
    while d < lax.axis_size("wide") // 2:
        v = (v.astype(F32) + swap_z(v, d).astype(F32)).astype(v.dtype)
        d *= 2
    return v


def sum_all(v):
    v = v + swap_core(v)
    v = v + swap_y(v)
    v = v + swap_x(v)
    return sum_z(v)


def spread_x(summed, x):
    rows = summed.shape[0] // 2
    keep = lax.dynamic_slice_in_dim(summed, x * rows, rows, 0)
    give = lax.dynamic_slice_in_dim(summed, (1 - x) * rows, rows, 0)
    return [keep, swap_x(give)]


def spread_y(pair):
    return pair + [swap_y(p) for p in pair]


def assemble_kernel(width, place, *refs):
    out = refs[GROUP]
    for r in range(GROUP):
        column = pl.multiple_of(place[r] * width, width)
        out[:, pl.ds(column, width)] = refs[r][...].astype(out.dtype)


def assemble(pieces, c, parts, dtype):
    rows = pieces[0].shape[0]
    width = pieces[0].shape[1] // parts
    r = jnp.arange(GROUP, dtype=jnp.int32)
    place = c ^ (((r >> 1) & 1) * 4 + ((r >> 2) & 1) * 2 + (r & 1))
    step = min(rows, (64 * 1024) // width)
    return pl.pallas_call(
        functools.partial(assemble_kernel, width),
        grid_spec=pltpu.PrefetchScalarGridSpec(
            num_scalar_prefetch=1,
            grid=(parts, rows // step),
            in_specs=[pl.BlockSpec((step, width), lambda p, i, o: (i, p))] * GROUP,
            out_specs=pl.BlockSpec((step, GROUP * width), lambda p, i, o: (i, p)),
        ),
        out_shape=jax.ShapeDtypeStruct((rows, parts * GROUP * width), dtype),
        compiler_params=pltpu.CompilerParams(vmem_limit_bytes=24 * 2**20),
    )(place, *pieces)


def assemble_stacked(stacked, c, dtype):
    rows, width = stacked.shape[0] // GROUP, stacked.shape[1]
    r = jnp.arange(GROUP, dtype=jnp.int32)
    place = c ^ (((r >> 1) & 1) * 4 + ((r >> 2) & 1) * 2 + (r & 1))
    return pl.pallas_call(
        functools.partial(assemble_kernel, width),
        grid_spec=pltpu.PrefetchScalarGridSpec(
            num_scalar_prefetch=1,
            grid=(1,),
            in_specs=[
                pl.BlockSpec((rows, width), lambda i, o, r=r: (r, 0)) for r in range(GROUP)
            ],
            out_specs=pl.BlockSpec((rows, GROUP * width), lambda i, o: (0, 0)),
        ),
        out_shape=jax.ShapeDtypeStruct((rows, GROUP * width), dtype),
        compiler_params=pltpu.CompilerParams(vmem_limit_bytes=24 * 2**20),
    )(place, *[stacked] * GROUP)


ROWS = 256


def masked_probs(queries, keys, first, scale):
    scores = lax.dot_general(
        queries, keys, (((1,), (1,)), ((), ())), preferred_element_type=F32
    ) * scale
    row = lax.broadcasted_iota(jnp.int32, scores.shape, 0) + first
    col = lax.broadcasted_iota(jnp.int32, scores.shape, 1)
    scores = jnp.where(col <= row, scores, -1e30)
    raised = jnp.exp(scores - jnp.max(scores, axis=-1, keepdims=True))
    return raised / jnp.sum(raised, axis=-1, keepdims=True)


def attention_kernel(scale, qkv_ref, out_ref):
    for first in range(0, SEG, ROWS):
        end = first + ROWS
        probs = masked_probs(qkv_ref[0, 0, first:end], qkv_ref[0, 1, :end], first, scale)
        out_ref[0, first:end] = jnp.dot(
            probs.astype(BF16), qkv_ref[0, 2, :end], preferred_element_type=F32
        )


def attention(qkv, scale):
    units = qkv.shape[0]
    return pl.pallas_call(
        functools.partial(attention_kernel, scale),
        grid=(units,),
        in_specs=[pl.BlockSpec((1, 3, SEG, DK), lambda u: (u, 0, 0, 0))],
        out_specs=pl.BlockSpec((1, SEG, DK), lambda u: (u, 0, 0)),
        out_shape=jax.ShapeDtypeStruct((units, SEG, DK), F32),
        compiler_params=pltpu.CompilerParams(vmem_limit_bytes=40 * 2**20),
        cost_estimate=pl.CostEstimate(
            flops=units * 4 * SEG * SEG * DK, bytes_accessed=units * SEG * DK * 10,
            transcendentals=units * SEG * SEG,
        ),
    )(qkv)


def attention_back_kernel(scale, qkv_ref, grad_ref, out_ref):
    out_ref[0, 1] = jnp.zeros((SEG, DK), F32)
    out_ref[0, 2] = jnp.zeros((SEG, DK), F32)
    for first in range(0, SEG, ROWS):
        end = first + ROWS
        queries, keys, values = qkv_ref[0, 0, first:end], qkv_ref[0, 1, :end], qkv_ref[0, 2, :end]
        grad = grad_ref[0, first:end]
        probs = masked_probs(queries, keys, first, scale)
        grad_probs = lax.dot_general(
            grad, values, (((1,), (1,)), ((), ())), preferred_element_type=F32
        )
        inner = jnp.sum(probs * grad_probs, axis=-1, keepdims=True)
        grad_scores = (probs * (grad_probs - inner)).astype(BF16)
        out_ref[0, 0, first:end] = jnp.dot(
            grad_scores, keys, preferred_element_type=F32
        ) * scale
        out_ref[0, 1, :end] += lax.dot_general(
            grad_scores, queries, (((0,), (0,)), ((), ())), preferred_element_type=F32
        )
        out_ref[0, 2, :end] += lax.dot_general(
            probs.astype(BF16), grad, (((0,), (0,)), ((), ())), preferred_element_type=F32
        )
    out_ref[0, 1] = out_ref[0, 1] * scale


def attention_back(qkv, grad, scale):
    units = qkv.shape[0]
    return pl.pallas_call(
        functools.partial(attention_back_kernel, scale),
        grid=(units,),
        in_specs=[
            pl.BlockSpec((1, 3, SEG, DK), lambda u: (u, 0, 0, 0)),
            pl.BlockSpec((1, SEG, DK), lambda u: (u, 0, 0)),
        ],
        out_specs=pl.BlockSpec((1, 3, SEG, DK), lambda u: (u, 0, 0, 0)),
        out_shape=jax.ShapeDtypeStruct((units, 3, SEG, DK), F32),
        compiler_params=pltpu.CompilerParams(vmem_limit_bytes=48 * 2**20),
        cost_estimate=pl.CostEstimate(
            flops=units * 10 * SEG * SEG * DK, bytes_accessed=units * SEG * DK * 20,
            transcendentals=units * SEG * SEG,
        ),
    )(qkv, grad)


def dot(a, b):
    return jnp.dot(a, b, preferred_element_type=F32)


def dot_t(a, b):
    return lax.dot_general(a, b, (((1,), (1,)), ((), ())), preferred_element_type=F32)


def t_dot(a, b):
    return lax.dot_general(a, b, (((0,), (0,)), ((), ())), preferred_element_type=F32)


def norm_back(grad_unit, unit_rows, scale_rows):
    return scale_rows * (
        grad_unit - unit_rows * jnp.mean(grad_unit * unit_rows, axis=-1, keepdims=True)
    )


def elu_slope(inputs):
    return jnp.where(inputs > 0, 1.0, jnp.exp(jnp.minimum(inputs, 0.0)))


def body(
    tokens,
    cotangent,
    qkv_weight,
    out_weight,
    gain_attn,
    gate_up_weight,
    down_weight,
    gain_mlp,
    gate_logit,
    memory_in,
    normalizer_in,
):
    wide = lax.axis_size("wide")
    n = lax.axis_index("narrow")
    w = lax.axis_index("wide")
    z, x = w // 2, w % 2
    c = n * 2 + x
    rows_here = tokens.shape[1]
    shard = qkv_weight.shape[0]
    span = SEG // rows_here
    zspan = span // 2
    zi = z % zspan
    segments = wide // span
    units = GROUP // zspan
    head_cols = D // GROUP
    ff_cols = FF // GROUP
    scale = DK ** (-0.5)

    first, _ = eighth_block(
        [(qkv_weight, 0, head_cols), (qkv_weight, D, head_cols), (qkv_weight, 2 * D, head_cols),
         (out_weight, 0, head_cols)], x, n
    )
    first_c = gather_rows(first)
    qkv_c = first_c[:, : 3 * head_cols]

    inputs = tokens[0].astype(F32)
    scale_one = lax.rsqrt(jnp.mean(inputs * inputs, axis=-1, keepdims=True) + EPSILON)
    unit_one = inputs * scale_one
    gains = gather_gains(jnp.stack([gain_attn, gain_mlp]), w).astype(F32)
    gain_one, gain_two = gains[0], gains[1]
    normed_one = (unit_one * gain_one).astype(BF16)
    one_pieces = plane(after(normed_one, first))

    gate_up_weight = after(gate_up_weight, one_pieces)
    gate_block, _ = eighth_block([(gate_up_weight, 0, ff_cols)], x, n)
    up_block, _ = eighth_block([(after(gate_up_weight, gate_block), FF, ff_cols)], x, n)
    down_block, _ = eighth_block([(after(down_weight, up_block), 0, ff_cols)], x, n)
    cot = cotangent[0]

    def to_units(own, other, parts):
        def split(flat):
            return flat.reshape(2, 2, rows_here, parts, 2, DK).transpose(1, 4, 0, 3, 2, 5)

        v = jnp.stack([split(own), split(other)], axis=2)
        v = by_bit([v[0], v[1]], x)
        v = v.transpose(1, 2, 3, 4, 0, 5, 6).reshape(GROUP, parts, 2 * rows_here, DK)
        blocks = []
        for d in range(zspan):
            block = lax.dynamic_slice_in_dim(v, (zi ^ d) * units, units, 0)
            given = block
            blocks.append(block if d == 0 else swap_z(block, d))
        v = by_index(blocks, zi)
        return v.transpose(1, 2, 0, 3, 4).reshape(units, parts, SEG, DK), given, blocks[-1]

    def from_units(v, parts):
        v = v.reshape(units, parts, zspan, 2 * rows_here, DK)
        blocks = []
        for d in range(zspan):
            block = lax.dynamic_slice_in_dim(v, zi ^ d, 1, 2)[:, :, 0]
            given = block
            blocks.append(block if d == 0 else swap_z(block, d))
        v = by_index(blocks, zi).reshape(2, 2, 2, parts, 2, rows_here, DK)
        v = by_bit([v[:, :, :, :, 0], v[:, :, :, :, 1]], x)
        v = v.transpose(2, 3, 0, 5, 4, 1, 6)
        return v.reshape(GROUP * rows_here, parts * head_cols), given, blocks[-1]

    half = 4 * rows_here
    one_all = join(both_cores(one_pieces))
    one_all, gate_block, up_block, down_block = lax.optimization_barrier(
        (one_all, gate_block, up_block, down_block)
    )
    projected = dot(one_all, qkv_c).astype(BF16)
    qkv_units, given, swapped = to_units(projected[:half], projected[half:], 3)
    gate_c = gather_rows(after(gate_block, swapped))
    out_pieces = plane(first_c[:, 3 * head_cols :])
    qkv_units, out_pieces = lax.optimization_barrier((qkv_units, out_pieces))
    out_full = assemble(both_cores(out_pieces), c, 1, BF16)
    queries, keys, values = qkv_units[:, 0], qkv_units[:, 1], qkv_units[:, 2]

    head_count = max(1, units // 4)
    seq_count = units // head_count
    first_head = (zi * units) // 4
    first_seq = (zi * units) % 4
    held = jnp.concatenate([memory_in[0], normalizer_in[0][:, None]], axis=1)
    fetched = []
    for offset in range(4):
        core, y = offset >> 1, offset & 1
        flip = y * 2 + core
        block = lax.dynamic_slice_in_dim(
            held, ((n ^ flip) * 2 + x) * 2 + first_head, head_count, 0
        )
        if flip:
            block = lax.ppermute(block, "narrow", [(i, i ^ flip) for i in range(4)])
        fetched.append(block)
    mem_in = jnp.stack(fetched, axis=1)
    mem_in = lax.dynamic_slice_in_dim(mem_in, first_seq, seq_count, 1)
    mem_in = mem_in.reshape(units, DK + 1, DK)

    query_f, key_f, value_f = (a.astype(F32) for a in (queries, keys, values))
    lift_q = jax.nn.elu(query_f) + 1.0
    lift_k = jax.nn.elu(key_f) + 1.0
    part_mem = jnp.einsum("utd,ute->ude", lift_k, value_f, preferred_element_type=F32)
    part_norm = jnp.sum(lift_k, axis=1)
    part = jnp.concatenate([part_mem, part_norm[:, None]], axis=1) / SEG
    direct = attention(after(qkv_units, part), scale)
    read = mem_in
    for k in range(1, segments):
        read = read + lax.ppermute(
            part, "wide", [(i, i + k * span) for i in range(wide - k * span)]
        )
    read_mem, read_norm = read[:, :DK], read[:, DK]
    numerator = jnp.einsum("utd,ude->ute", lift_q, read_mem, preferred_element_type=F32)
    denominator = jnp.sum(lift_q * read_norm[:, None], axis=-1, keepdims=True)
    recalled = numerator / denominator

    unit_heads = c * 2 + (zi * units + jnp.arange(units)) // 4
    mixing = jax.nn.sigmoid(gate_logit[unit_heads])
    mix = mixing[:, None, None]
    attended_units = (mix * recalled + (1.0 - mix) * direct).astype(BF16)
    attended_c, given, swapped = from_units(attended_units[:, None], 1)
    up_c = gather_rows(after(up_block, swapped))
    down_c = gather_rows(after(down_block, swapped))
    attended_c, out_full = lax.optimization_barrier((attended_c, out_full))
    attended_c = attended_c.reshape(GROUP, rows_here, head_cols)
    sent = exchange_group([attended_c[r] for r in range(GROUP)])
    attended = assemble_stacked(jnp.concatenate(sent, axis=0), c, BF16)

    middle = inputs + dot(attended, out_full)
    scale_two = lax.rsqrt(jnp.mean(middle * middle, axis=-1, keepdims=True) + EPSILON)
    unit_two = middle * scale_two
    normed_two = (unit_two * gain_two).astype(BF16)
    two_pieces = plane(normed_two)
    cot_pieces = plane(after(cot, two_pieces))
    two_all = join(both_cores(two_pieces))
    gate_short = dot(two_all, gate_c).astype(BF16)
    up_short = dot(after(two_all, gate_short), up_c).astype(BF16)
    cot_pieces, up_short, down_c = lax.optimization_barrier((cot_pieces, up_short, down_c))
    gate_part, up_part = gate_short.astype(F32), up_short.astype(F32)
    gate_sig = jax.nn.sigmoid(gate_part)
    activation = (gate_part * gate_sig * up_part).astype(BF16)
    cot_all = join(both_cores(cot_pieces))
    grad_down_part = t_dot(cot_all, activation).astype(BF16)
    grad_down_c = reduce_rows(grad_down_part)
    att_pieces = plane(after(attended, cot_all))
    grad_activ = dot(after(cot_all, grad_down_part), down_c)
    grad_gate = (
        grad_activ * up_part * gate_sig * (1.0 + gate_part * (1.0 - gate_sig))
    ).astype(BF16)
    grad_upper = (grad_activ * gate_part * gate_sig).astype(BF16)
    back = (dot_t(grad_gate, gate_c) + dot_t(grad_upper, up_c)).astype(BF16)
    back, att_pieces = lax.optimization_barrier((back, att_pieces))
    back_got = scatter_sends(scatter_start(back))
    grad_gate_part = t_dot(two_all, after(grad_gate, back)).astype(BF16)
    grad_gate_c = reduce_rows(grad_gate_part)
    grad_up_part = t_dot(two_all, after(grad_upper, grad_gate_part)).astype(BF16)
    grad_up_c = reduce_rows(grad_up_part)
    mlp_part = dot_t(after(activation, grad_up_part), down_c).astype(BF16)
    att_all = join(both_cores(att_pieces))
    mlp_sums = scatter_start(mlp_part)
    back_got, mlp_sums, att_all, grad_down_c = lax.optimization_barrier(
        (back_got, mlp_sums, att_all, grad_down_c)
    )
    mlp_got = scatter_sends(mlp_sums)
    grad_normed_two = scatter_total(back_got)
    grad_gain_two = jnp.sum(grad_normed_two * unit_two, axis=0)
    grad_middle = cot.astype(F32) + norm_back(grad_normed_two * gain_two, unit_two, scale_two)

    grad_branch = grad_middle.astype(BF16)
    grad_att_rows = dot_t(grad_branch, out_full).astype(BF16)
    sent = exchange_group(
        [
            lax.dynamic_slice_in_dim(grad_att_rows, (c ^ absolute(r)) * head_cols, head_cols, 1)
            for r in range(GROUP)
        ]
    )
    sent, mlp_got = lax.optimization_barrier((sent, mlp_got))
    grad_att_units, given, _ = to_units(
        jnp.concatenate(sent[:4], axis=0), jnp.concatenate(sent[4:], axis=0), 1
    )

    late_branch, late_down = after((grad_branch, grad_down_c), given)
    branch_pieces = exchange_group(
        [
            lax.dynamic_slice_in_dim(late_branch, (c ^ absolute(r)) * head_cols, head_cols, 1)
            for r in range(GROUP)
        ]
    )
    down_pair = spread_x(late_down, x)
    grad_att_units, branch_pieces = lax.optimization_barrier((grad_att_units, branch_pieces))
    grad_att = grad_att_units[:, 0].astype(F32)

    unit_logit = jnp.sum(grad_att * (recalled - direct), axis=(1, 2)) * mixing * (1.0 - mixing)
    grad_logit = jnp.sum(
        jnp.where(unit_heads[:, None] == jnp.arange(H)[None], unit_logit[:, None], 0.0), axis=0
    )
    grad_recall = (mix * grad_att).astype(BF16).astype(F32)
    grad_numer = grad_recall / denominator
    grad_denom = -jnp.sum(grad_recall * recalled, axis=-1, keepdims=True) / denominator
    grad_lift_q = (
        jnp.einsum("ute,ude->utd", grad_numer, read_mem, preferred_element_type=F32)
        + grad_denom * read_norm[:, None]
    )
    grad_read_mem = jnp.einsum("utd,ute->ude", lift_q, grad_numer, preferred_element_type=F32)
    grad_read_norm = jnp.sum(grad_denom * lift_q, axis=1)
    grad_read = jnp.concatenate([grad_read_mem, grad_read_norm[:, None]], axis=1)
    grad_direct = after((1.0 - mix) * grad_att, grad_read).astype(BF16)
    dots = attention_back(qkv_units, grad_direct, scale)
    later = jnp.zeros_like(grad_read)
    for k in range(1, segments):
        later = later + lax.ppermute(
            grad_read, "wide", [(i + k * span, i) for i in range(wide - k * span)]
        )
    later, dots, down_pair = lax.optimization_barrier((later / SEG, dots, down_pair))
    down_four = spread_y(down_pair)
    gate_up_pair = spread_x(
        jnp.concatenate(after([grad_gate_c, grad_up_c], dots), axis=1), x
    )
    grad_q_dot, grad_k_dot, grad_v_dot = dots[:, 0], dots[:, 1], dots[:, 2]
    later_mem, later_norm = later[:, :DK], later[:, DK]
    grad_lift_k = (
        jnp.einsum("ute,ude->utd", value_f, later_mem, preferred_element_type=F32)
        + later_norm[:, None]
    )
    grad_v_mem = jnp.einsum("utd,ude->ute", lift_k, later_mem, preferred_element_type=F32)
    grad_units = jnp.stack(
        [
            grad_q_dot + grad_lift_q * elu_slope(query_f),
            grad_k_dot + grad_lift_k * elu_slope(key_f),
            grad_v_dot + grad_v_mem,
        ],
        axis=1,
    ).astype(BF16)
    grad_projected, given, _ = from_units(grad_units, 3)
    grad_out_part = t_dot(
        after(att_all, given), jnp.concatenate(branch_pieces, axis=0)
    ).astype(BF16)
    grad_out_c = reduce_rows(grad_out_part)
    grad_projected, grad_out_part, down_four, gate_up_pair = lax.optimization_barrier(
        (grad_projected, grad_out_part, down_four, gate_up_pair)
    )
    grad_qkv_part = t_dot(one_all, grad_projected).astype(BF16)
    grad_qkv_c = reduce_rows(grad_qkv_part)
    one_part = dot_t(after(grad_projected, grad_qkv_part), qkv_c).astype(BF16)
    gate_up_y = swap_y(gate_up_pair[0])
    one_part, gate_up_y = lax.optimization_barrier((one_part, gate_up_y))
    one_sums = scatter_start(one_part)
    one_got = scatter_sends(one_sums)
    gate_up_four = gate_up_pair + [gate_up_y, swap_y(after(gate_up_pair[1], gate_up_y))]
    grad_down = assemble(both_cores(after(down_four, one_sums)), c, 1, F32)
    output = (middle + scatter_total(after(mlp_got, one_sums))).astype(BF16)[None]
    one_got, gate_up_four, grad_down, output = lax.optimization_barrier(
        (one_got, gate_up_four, grad_down, output)
    )
    grad_normed_one = scatter_total(one_got)
    grad_gain_one = jnp.sum(grad_normed_one * unit_one, axis=0)
    grad_tokens = (
        grad_middle + norm_back(grad_normed_one * gain_one, unit_one, scale_one)
    ).astype(BF16)[None]
    def finish(four, parts):
        return assemble(both_cores(four), c, parts, F32)

    out_four = spread_y(spread_x(after(grad_out_c, gate_up_four), x))
    grad_gate_up = finish(gate_up_four, 2)
    qkv_pair = spread_x(after(grad_qkv_c, out_four, grad_normed_one), x)
    qkv_four = spread_y(qkv_pair)
    grad_out = finish(out_four, 1)
    grad_qkv = finish(qkv_four, 3)

    placed = jnp.zeros((GROUP, DK + 1, DK), BF16)
    placed = lax.dynamic_update_slice_in_dim(placed, after(grad_read, one_sums).astype(BF16), zi * units, 0)
    placed = placed.reshape(2, 4, DK + 1, DK)
    got = []
    for flip in range(4):
        core, y = flip & 1, flip >> 1
        block = placed[:, core * 2 + y]
        if flip:
            block = lax.ppermute(block, "narrow", [(i, i ^ flip) for i in range(4)])
        got.append(block)
    mine = sum_z(by_index(after(got, grad_normed_one), n))
    heads = by_bit([mine, swap_x(mine)], x).transpose(1, 0, 2, 3, 4)
    heads = heads.reshape(H, DK + 1, DK).astype(F32)

    small = sum_all(jnp.concatenate([grad_gain_one, grad_gain_two, grad_logit]))
    gain_one_sum = lax.dynamic_slice_in_dim(small, w * shard, shard, 0)
    gain_two_sum = lax.dynamic_slice_in_dim(small, D + w * shard, shard, 0)
    return (
        output,
        grad_tokens,
        heads[None, :, :DK],
        heads[None, :, DK],
        grad_qkv,
        grad_out,
        gain_one_sum,
        grad_gate_up,
        grad_down,
        gain_two_sum,
        small[2 * D :],
    )


def solution(mesh):
    return jax.shard_map(
        body,
        mesh=mesh,
        in_specs=(
            P("narrow", "wide", None),
            P("narrow", "wide", None),
            P("wide", None),
            P("wide", None),
            P("wide"),
            P("wide", None),
            P("wide", None),
            P("wide"),
            P(),
            P("narrow", None, None, None),
            P("narrow", None, None),
        ),
        out_specs=(
            P("narrow", "wide", None),
            P("narrow", "wide", None),
            P("narrow", None, None, None),
            P("narrow", None, None),
            P("wide", None),
            P("wide", None),
            P("wide"),
            P("wide", None),
            P("wide", None),
            P("wide"),
            P(),
        ),
        check_vma=False,
    )
```

```python
import functools

import jax
import jax.numpy as jnp
from jax import lax
from jax.experimental import pallas as pl
from jax.experimental.pallas import tpu as pltpu
from jax.sharding import PartitionSpec as P

D = 2048
H = 16
DK = 128
FF = 8192
SEG = 1024
EPSILON = 1e-06
F32 = jnp.float32
BF16 = jnp.bfloat16
GROUP = 8


def swap_x(v):
    n = lax.axis_size("wide")
    return lax.ppermute(v, "wide", [(i, i ^ 1) for i in range(n)])


def swap_y(v):
    return lax.ppermute(v, "narrow", [(i, i ^ 2) for i in range(4)])


def swap_core(v):
    return lax.ppermute(v, "narrow", [(i, i ^ 1) for i in range(4)])


def swap_z(v, d):
    n = lax.axis_size("wide")
    return lax.ppermute(v, "wide", [(i, i ^ (2 * d)) for i in range(n)])


def offset_bits(r):
    return (r >> 1) & 1, (r >> 2) & 1, r & 1


def absolute(r):
    y, core, x = offset_bits(r)
    return y * 4 + core * 2 + x


def send_offset(v, r):
    y, core, x = offset_bits(r)
    n = lax.axis_size("wide")
    flip = y * 2 + core
    route = [(a * n + b, (a ^ flip) * n + (b ^ x)) for a in range(4) for b in range(n)]
    return lax.ppermute(v, ("narrow", "wide"), route)


def plane(v):
    return [v] + [send_offset(v, r) for r in range(1, 4)]


def both_cores(pieces):
    return pieces + [swap_core(p) for p in pieces]


def scatter_start(partial):
    rows = partial.shape[0] // GROUP
    parts = [partial[r * rows : (r + 1) * rows] for r in range(GROUP)]
    sums = [None] * 4
    for r in (3, 1, 2, 0):
        sums[r] = parts[r].astype(F32) + swap_core(parts[4 + r]).astype(F32)
    return [sums[0]] + [v.astype(BF16) for v in sums[1:]]


def scatter_sends(sums):
    return [sums[0]] + [send_offset(sums[r], r) for r in range(1, 4)]


def scatter_total(got):
    return got[0] + got[1].astype(F32) + got[2].astype(F32) + got[3].astype(F32)


def join_kernel(*refs):
    out = refs[-1]
    rows = refs[0].shape[0]
    for i, piece in enumerate(refs[:-1]):
        out[i * rows : (i + 1) * rows] = piece[...]


def join(pieces):
    rows, columns = pieces[0].shape
    step = min(columns, 512)
    return pl.pallas_call(
        join_kernel,
        grid=(columns // step,),
        in_specs=[pl.BlockSpec((rows, step), lambda j: (0, j))] * len(pieces),
        out_specs=pl.BlockSpec((len(pieces) * rows, step), lambda j: (0, j)),
        out_shape=jax.ShapeDtypeStruct((len(pieces) * rows, columns), pieces[0].dtype),
        compiler_params=pltpu.CompilerParams(vmem_limit_bytes=24 * 2**20),
    )(*pieces)


def exchange_group(blocks):
    return lax.optimization_barrier(
        [blocks[0]] + [send_offset(blocks[r], r) for r in range(1, GROUP)]
    )


def by_bit(pair, bit):
    a, b = pair
    return jnp.where(bit == 0, jnp.stack([a, b]), jnp.stack([b, a]))


def by_index(parts, index):
    if len(parts) == 2:
        return by_bit(parts, index)
    out = jnp.zeros((len(parts),) + parts[0].shape, parts[0].dtype)
    for d, part in enumerate(parts):
        out = lax.dynamic_update_slice_in_dim(out, part[None], index ^ d, 0)
    return out


def after(v, *others):
    return lax.optimization_barrier((v, others))[0]


def z_lines():
    n = lax.axis_size("wide")
    return [list(range(x, n, 2)) for x in range(2)]


def eighth_block(parts, x, n):
    c = n * 2 + x

    def columns(eighth):
        return jnp.concatenate(
            [lax.dynamic_slice_in_dim(a, s + eighth * m, m, 1) for a, s, m in parts], axis=1
        )

    give = columns(c ^ 1)
    pair = by_bit([columns(c), swap_x(give)], x)
    return pair.reshape(pair.shape[0] * pair.shape[1], -1), give


def gather_rows(block):
    return lax.all_gather(block, "wide", axis=0, tiled=True, axis_index_groups=z_lines())


def plane_groups():
    n = lax.axis_size("wide")
    return [[a * n + z * 2 + x for a in range(4) for x in range(2)] for z in range(n // 2)]


def reduce_rows(partial):
    return lax.psum_scatter(
        partial, "wide", scatter_dimension=0, tiled=True, axis_index_groups=z_lines()
    )


def gather_gains(v, w):
    n = lax.axis_size("wide")
    blocks = [v]
    for d in range(1, n):
        blocks.append(lax.ppermute(v, "wide", [(i, i ^ d) for i in range(n)]))
    return by_index(blocks, w).transpose(1, 0, 2).reshape(2, -1)


def sum_z(v):
    d = 1
    while d < lax.axis_size("wide") // 2:
        v = (v.astype(F32) + swap_z(v, d).astype(F32)).astype(v.dtype)
        d *= 2
    return v


def sum_all(v):
    v = v + swap_core(v)
    v = v + swap_y(v)
    v = v + swap_x(v)
    return sum_z(v)


def spread_x(summed, x):
    rows = summed.shape[0] // 2
    keep = lax.dynamic_slice_in_dim(summed, x * rows, rows, 0)
    give = lax.dynamic_slice_in_dim(summed, (1 - x) * rows, rows, 0)
    return [keep, swap_x(give)]


def spread_y(pair):
    return pair + [swap_y(p) for p in pair]


def reorder_kernel(order, in_ref, out_ref):
    del order
    out_ref[...] = in_ref[...]


def reorder(rows_by_offset, c):
    rows, columns = rows_by_offset.shape[0] // GROUP, rows_by_offset.shape[1]
    d = c ^ jnp.arange(GROUP, dtype=jnp.int32)
    order = ((d >> 1) & 1) * 4 + ((d >> 2) & 1) * 2 + (d & 1)
    return pl.pallas_call(
        reorder_kernel,
        grid_spec=pltpu.PrefetchScalarGridSpec(
            num_scalar_prefetch=1,
            grid=(GROUP,),
            in_specs=[pl.BlockSpec((rows, columns), lambda i, o: (o[i], 0))],
            out_specs=pl.BlockSpec((rows, columns), lambda i, o: (i, 0)),
        ),
        out_shape=jax.ShapeDtypeStruct(rows_by_offset.shape, rows_by_offset.dtype),
        compiler_params=pltpu.CompilerParams(vmem_limit_bytes=24 * 2**20),
    )(order, rows_by_offset)


def assemble_kernel(width, place, *refs):
    out = refs[GROUP]
    for r in range(GROUP):
        column = pl.multiple_of(place[r] * width, width)
        out[:, pl.ds(column, width)] = refs[r][...].astype(out.dtype)


def assemble(pieces, c, parts, dtype):
    rows = pieces[0].shape[0]
    width = pieces[0].shape[1] // parts
    r = jnp.arange(GROUP, dtype=jnp.int32)
    place = c ^ (((r >> 1) & 1) * 4 + ((r >> 2) & 1) * 2 + (r & 1))
    step = min(rows, (64 * 1024) // width)
    return pl.pallas_call(
        functools.partial(assemble_kernel, width),
        grid_spec=pltpu.PrefetchScalarGridSpec(
            num_scalar_prefetch=1,
            grid=(parts, rows // step),
            in_specs=[pl.BlockSpec((step, width), lambda p, i, o: (i, p))] * GROUP,
            out_specs=pl.BlockSpec((step, GROUP * width), lambda p, i, o: (i, p)),
        ),
        out_shape=jax.ShapeDtypeStruct((rows, parts * GROUP * width), dtype),
        compiler_params=pltpu.CompilerParams(vmem_limit_bytes=24 * 2**20),
    )(place, *pieces)


def assemble_stacked(stacked, c, dtype):
    rows, width = stacked.shape[0] // GROUP, stacked.shape[1]
    r = jnp.arange(GROUP, dtype=jnp.int32)
    place = c ^ (((r >> 1) & 1) * 4 + ((r >> 2) & 1) * 2 + (r & 1))
    return pl.pallas_call(
        functools.partial(assemble_kernel, width),
        grid_spec=pltpu.PrefetchScalarGridSpec(
            num_scalar_prefetch=1,
            grid=(1,),
            in_specs=[
                pl.BlockSpec((rows, width), lambda i, o, r=r: (r, 0)) for r in range(GROUP)
            ],
            out_specs=pl.BlockSpec((rows, GROUP * width), lambda i, o: (0, 0)),
        ),
        out_shape=jax.ShapeDtypeStruct((rows, GROUP * width), dtype),
        compiler_params=pltpu.CompilerParams(vmem_limit_bytes=24 * 2**20),
    )(place, *[stacked] * GROUP)


def pack_kernel(parts, where, in_ref, keep_ref, give_ref):
    for part in range(parts):
        keep = pl.multiple_of(part * 2 * DK + where[1] * DK, DK)
        give = pl.multiple_of(part * 2 * DK + (1 - where[1]) * DK, DK)
        keep_ref[0, part] = in_ref[:, pl.ds(keep, DK)]
        give_ref[0, part] = in_ref[:, pl.ds(give, DK)]


def pack(flat, x, zi):
    step = flat.shape[0] // GROUP
    parts = flat.shape[1] // (2 * DK)
    block = pl.BlockSpec((1, parts, step, DK), lambda u, d, w: (u, 0, w[0] ^ d, 0))
    shape = jax.ShapeDtypeStruct((4, parts, 2 * step, DK), flat.dtype)
    return pl.pallas_call(
        functools.partial(pack_kernel, parts),
        grid_spec=pltpu.PrefetchScalarGridSpec(
            num_scalar_prefetch=1,
            grid=(4, 2),
            in_specs=[pl.BlockSpec((step, parts * 2 * DK), lambda u, d, w: (u * 2 + d, 0))],
            out_specs=[block, block],
        ),
        out_shape=[shape, shape],
        compiler_params=pltpu.CompilerParams(vmem_limit_bytes=24 * 2**20),
    )(jnp.stack([x, zi]).astype(jnp.int32), flat)


def unpack_kernel(parts, where, own_ref, other_ref, out_ref):
    for part in range(parts):
        own = pl.multiple_of(part * 2 * DK + where[1] * DK, DK)
        other = pl.multiple_of(part * 2 * DK + (1 - where[1]) * DK, DK)
        out_ref[:, pl.ds(own, DK)] = own_ref[0, part]
        out_ref[:, pl.ds(other, DK)] = other_ref[0, part]


def unpack(own, other, x, zi):
    units, parts, rows = own.shape[:3]
    step = rows // 2
    block = pl.BlockSpec((1, parts, step, DK), lambda u, d, w: (u, 0, w[0] ^ d, 0))
    return pl.pallas_call(
        functools.partial(unpack_kernel, parts),
        grid_spec=pltpu.PrefetchScalarGridSpec(
            num_scalar_prefetch=1,
            grid=(units, 2),
            in_specs=[block, block],
            out_specs=pl.BlockSpec((step, parts * 2 * DK), lambda u, d, w: (u * 2 + d, 0)),
        ),
        out_shape=jax.ShapeDtypeStruct((units * rows, parts * 2 * DK), own.dtype),
        compiler_params=pltpu.CompilerParams(vmem_limit_bytes=24 * 2**20),
    )(jnp.stack([x, zi]).astype(jnp.int32), own, other)


ROWS = 256


def masked_probs(queries, keys, first, scale):
    scores = lax.dot_general(
        queries, keys, (((1,), (1,)), ((), ())), preferred_element_type=F32
    ) * scale
    row = lax.broadcasted_iota(jnp.int32, scores.shape, 0) + first
    col = lax.broadcasted_iota(jnp.int32, scores.shape, 1)
    scores = jnp.where(col <= row, scores, -1e30)
    raised = jnp.exp(scores - jnp.max(scores, axis=-1, keepdims=True))
    return raised / jnp.sum(raised, axis=-1, keepdims=True)


def attention_kernel(scale, qkv_ref, out_ref):
    for first in range(0, SEG, ROWS):
        end = first + ROWS
        probs = masked_probs(qkv_ref[0, 0, first:end], qkv_ref[0, 1, :end], first, scale)
        out_ref[0, first:end] = jnp.dot(
            probs.astype(BF16), qkv_ref[0, 2, :end], preferred_element_type=F32
        )


def attention(qkv, scale):
    units = qkv.shape[0]
    return pl.pallas_call(
        functools.partial(attention_kernel, scale),
        grid=(units,),
        in_specs=[pl.BlockSpec((1, 3, SEG, DK), lambda u: (u, 0, 0, 0))],
        out_specs=pl.BlockSpec((1, SEG, DK), lambda u: (u, 0, 0)),
        out_shape=jax.ShapeDtypeStruct((units, SEG, DK), F32),
        compiler_params=pltpu.CompilerParams(vmem_limit_bytes=40 * 2**20),
        cost_estimate=pl.CostEstimate(
            flops=units * 4 * SEG * SEG * DK, bytes_accessed=units * SEG * DK * 10,
            transcendentals=units * SEG * SEG,
        ),
    )(qkv)


def attention_back_kernel(scale, qkv_ref, grad_ref, out_ref):
    out_ref[0, 1] = jnp.zeros((SEG, DK), F32)
    out_ref[0, 2] = jnp.zeros((SEG, DK), F32)
    for first in range(0, SEG, ROWS):
        end = first + ROWS
        queries, keys, values = qkv_ref[0, 0, first:end], qkv_ref[0, 1, :end], qkv_ref[0, 2, :end]
        grad = grad_ref[0, first:end]
        probs = masked_probs(queries, keys, first, scale)
        grad_probs = lax.dot_general(
            grad, values, (((1,), (1,)), ((), ())), preferred_element_type=F32
        )
        inner = jnp.sum(probs * grad_probs, axis=-1, keepdims=True)
        grad_scores = (probs * (grad_probs - inner)).astype(BF16)
        out_ref[0, 0, first:end] = jnp.dot(
            grad_scores, keys, preferred_element_type=F32
        ) * scale
        out_ref[0, 1, :end] += lax.dot_general(
            grad_scores, queries, (((0,), (0,)), ((), ())), preferred_element_type=F32
        )
        out_ref[0, 2, :end] += lax.dot_general(
            probs.astype(BF16), grad, (((0,), (0,)), ((), ())), preferred_element_type=F32
        )
    out_ref[0, 1] = out_ref[0, 1] * scale


def attention_back(qkv, grad, scale):
    units = qkv.shape[0]
    return pl.pallas_call(
        functools.partial(attention_back_kernel, scale),
        grid=(units,),
        in_specs=[
            pl.BlockSpec((1, 3, SEG, DK), lambda u: (u, 0, 0, 0)),
            pl.BlockSpec((1, SEG, DK), lambda u: (u, 0, 0)),
        ],
        out_specs=pl.BlockSpec((1, 3, SEG, DK), lambda u: (u, 0, 0, 0)),
        out_shape=jax.ShapeDtypeStruct((units, 3, SEG, DK), F32),
        compiler_params=pltpu.CompilerParams(vmem_limit_bytes=48 * 2**20),
        cost_estimate=pl.CostEstimate(
            flops=units * 10 * SEG * SEG * DK, bytes_accessed=units * SEG * DK * 20,
            transcendentals=units * SEG * SEG,
        ),
    )(qkv, grad)


def dot(a, b):
    return jnp.dot(a, b, preferred_element_type=F32)


def dot_t(a, b):
    return lax.dot_general(a, b, (((1,), (1,)), ((), ())), preferred_element_type=F32)


def t_dot(a, b):
    return lax.dot_general(a, b, (((0,), (0,)), ((), ())), preferred_element_type=F32)


def norm_back(grad_unit, unit_rows, scale_rows):
    return scale_rows * (
        grad_unit - unit_rows * jnp.mean(grad_unit * unit_rows, axis=-1, keepdims=True)
    )


def elu_slope(inputs):
    return jnp.where(inputs > 0, 1.0, jnp.exp(jnp.minimum(inputs, 0.0)))


def body(
    tokens,
    cotangent,
    qkv_weight,
    out_weight,
    gain_attn,
    gate_up_weight,
    down_weight,
    gain_mlp,
    gate_logit,
    memory_in,
    normalizer_in,
):
    wide = lax.axis_size("wide")
    n = lax.axis_index("narrow")
    w = lax.axis_index("wide")
    z, x = w // 2, w % 2
    c = n * 2 + x
    rows_here = tokens.shape[1]
    shard = qkv_weight.shape[0]
    span = SEG // rows_here
    zspan = span // 2
    zi = z % zspan
    segments = wide // span
    units = GROUP // zspan
    head_cols = D // GROUP
    ff_cols = FF // GROUP
    scale = DK ** (-0.5)

    first, _ = eighth_block(
        [(qkv_weight, 0, head_cols), (qkv_weight, D, head_cols), (qkv_weight, 2 * D, head_cols),
         (out_weight, 0, head_cols)], x, n
    )
    first_c = gather_rows(first)
    qkv_c = first_c[:, : 3 * head_cols]

    inputs = tokens[0].astype(F32)
    scale_one = lax.rsqrt(jnp.mean(inputs * inputs, axis=-1, keepdims=True) + EPSILON)
    unit_one = inputs * scale_one
    gains = gather_gains(jnp.stack([gain_attn, gain_mlp]), w).astype(F32)
    gain_one, gain_two = gains[0], gains[1]
    normed_one = (unit_one * gain_one).astype(BF16)
    one_pieces = plane(after(normed_one, first))

    cot = cotangent[0]

    def to_units(flat, parts, beside=()):
        if zspan == 2:
            keep, given = pack(flat, x, zi)
            blocks = [keep, swap_z(given, 1)]
        else:
            v = flat.reshape(2, 2, 2, rows_here, parts, 2, DK).transpose(2, 5, 0, 1, 4, 3, 6)
            v = by_bit([v[0], v[1]], x)
            v = v.transpose(1, 2, 3, 4, 0, 5, 6).reshape(GROUP, parts, 2 * rows_here, DK)
            blocks = []
            for d in range(zspan):
                block = lax.dynamic_slice_in_dim(v, (zi ^ d) * units, units, 0)
                given = block
                blocks.append(block if d == 0 else swap_z(block, d))
        if callable(beside):
            beside = beside(given)
        blocks, beside = lax.optimization_barrier((blocks, beside))
        v = by_index(blocks, zi)
        return v.transpose(1, 2, 0, 3, 4).reshape(units, parts, SEG, DK), given, blocks[-1], beside

    def from_units(v, parts, beside=()):
        v = v.reshape(units, parts, zspan, 2 * rows_here, DK)
        blocks = []
        for d in range(zspan):
            block = lax.dynamic_slice_in_dim(v, zi ^ d, 1, 2)[:, :, 0]
            given = block
            blocks.append(block if d == 0 else swap_z(block, d))
        if callable(beside):
            beside = beside(given)
        blocks, beside = lax.optimization_barrier((blocks, beside))
        if zspan == 2:
            return unpack(blocks[0], blocks[1], x, zi), blocks[-1], beside
        v = by_index(blocks, zi).reshape(2, 2, 2, parts, 2, rows_here, DK)
        v = by_bit([v[:, :, :, :, 0], v[:, :, :, :, 1]], x)
        v = v.transpose(2, 3, 0, 5, 4, 1, 6)
        return v.reshape(GROUP * rows_here, parts * head_cols), blocks[-1], beside

    one_all = join(both_cores(one_pieces))
    projected = dot(one_all, qkv_c).astype(BF16)

    def late_blocks(given):
        late_weight = after(gate_up_weight, given)
        return [eighth_block([(late_weight, s, ff_cols)], x, n)[0] for s in (0, FF)]

    qkv_units, given, swapped, (gate_block, up_block) = to_units(
        projected, 3, late_blocks
    )
    gate_c = gather_rows(after(gate_block, swapped))
    up_c = gather_rows(after(up_block, swapped))
    queries, keys, values = qkv_units[:, 0], qkv_units[:, 1], qkv_units[:, 2]

    head_count = max(1, units // 4)
    seq_count = units // head_count
    first_head = (zi * units) // 4
    first_seq = (zi * units) % 4
    held = jnp.concatenate([memory_in[0], normalizer_in[0][:, None]], axis=1)
    fetched = []
    for offset in range(4):
        core, y = offset >> 1, offset & 1
        flip = y * 2 + core
        block = lax.dynamic_slice_in_dim(
            held, ((n ^ flip) * 2 + x) * 2 + first_head, head_count, 0
        )
        if flip:
            block = lax.ppermute(block, "narrow", [(i, i ^ flip) for i in range(4)])
        fetched.append(block)
    mem_in = jnp.stack(fetched, axis=1)
    mem_in = lax.dynamic_slice_in_dim(mem_in, first_seq, seq_count, 1)
    mem_in = mem_in.reshape(units, DK + 1, DK)

    query_f, key_f, value_f = (a.astype(F32) for a in (queries, keys, values))
    lift_q = jax.nn.elu(query_f) + 1.0
    lift_k = jax.nn.elu(key_f) + 1.0
    part_mem = jnp.einsum("utd,ute->ude", lift_k, value_f, preferred_element_type=F32)
    part_norm = jnp.sum(lift_k, axis=1)
    part = jnp.concatenate([part_mem, part_norm[:, None]], axis=1) / SEG
    direct = attention(after(qkv_units, part), scale)
    read = mem_in
    for k in range(1, segments):
        read = read + lax.ppermute(
            part, "wide", [(i, i + k * span) for i in range(wide - k * span)]
        )
    read_mem, read_norm = read[:, :DK], read[:, DK]
    numerator = jnp.einsum("utd,ude->ute", lift_q, read_mem, preferred_element_type=F32)
    denominator = jnp.sum(lift_q * read_norm[:, None], axis=-1, keepdims=True)
    recalled = numerator / denominator

    unit_heads = c * 2 + (zi * units + jnp.arange(units)) // 4
    mixing = jax.nn.sigmoid(gate_logit[unit_heads])
    mix = mixing[:, None, None]
    attended_units = (mix * recalled + (1.0 - mix) * direct).astype(BF16)

    def late_out(given):
        out_late, down_late = after((first_c[:, 3 * head_cols :], down_weight), given)
        return plane(out_late), eighth_block([(down_late, 0, ff_cols)], x, n)[0]

    attended_c, swapped, (out_pieces, down_block) = from_units(
        attended_units[:, None], 1, late_out
    )
    down_c = gather_rows(down_block)
    attended_c = attended_c.reshape(GROUP, rows_here, head_cols)
    sent = exchange_group([attended_c[r] for r in range(GROUP)])
    out_full = assemble(both_cores(out_pieces), c, 1, BF16)
    attended = assemble_stacked(jnp.concatenate(sent, axis=0), c, BF16)

    middle = inputs + dot(attended, out_full)
    scale_two = lax.rsqrt(jnp.mean(middle * middle, axis=-1, keepdims=True) + EPSILON)
    unit_two = middle * scale_two
    normed_two = (unit_two * gain_two).astype(BF16)
    two_pieces = plane(normed_two)
    cot_pieces = plane(after(cot, two_pieces))
    two_all = join(both_cores(two_pieces))
    gate_short = dot(two_all, gate_c).astype(BF16)
    up_short = dot(after(two_all, gate_short), up_c).astype(BF16)
    cot_pieces, up_short = lax.optimization_barrier((cot_pieces, up_short))
    gate_part, up_part = gate_short.astype(F32), up_short.astype(F32)
    gate_sig = jax.nn.sigmoid(gate_part)
    activation = (gate_part * gate_sig * up_part).astype(BF16)
    cot_all = join(both_cores(cot_pieces))
    grad_down_part = t_dot(cot_all, activation).astype(BF16)
    grad_down_c = reduce_rows(grad_down_part)
    att_pieces = plane(after(attended, cot_all))
    grad_activ = dot(after(cot_all, grad_down_part), down_c)
    grad_gate = (
        grad_activ * up_part * gate_sig * (1.0 + gate_part * (1.0 - gate_sig))
    ).astype(BF16)
    grad_upper = (grad_activ * gate_part * gate_sig).astype(BF16)
    back = (dot_t(grad_gate, gate_c) + dot_t(grad_upper, up_c)).astype(BF16)
    back, att_pieces = lax.optimization_barrier((back, att_pieces))
    grad_gate_part = t_dot(two_all, after(grad_gate, back)).astype(BF16)
    back_sums, grad_gate_part = lax.optimization_barrier((scatter_start(back), grad_gate_part))
    back_got = scatter_sends(back_sums)
    grad_gate_c = reduce_rows(grad_gate_part)
    grad_up_part = t_dot(two_all, after(grad_upper, grad_gate_part)).astype(BF16)
    grad_up_c = reduce_rows(grad_up_part)
    mlp_part = reorder(dot_t(after(activation, grad_up_part), down_c).astype(BF16), c)
    back_got, mlp_part, grad_down_c = lax.optimization_barrier(
        (back_got, mlp_part, grad_down_c)
    )
    grad_normed_two = scatter_total(back_got)
    grad_gain_two = jnp.sum(grad_normed_two * unit_two, axis=0)
    grad_middle = cot.astype(F32) + norm_back(grad_normed_two * gain_two, unit_two, scale_two)

    grad_branch = grad_middle.astype(BF16)
    grad_att_rows = dot_t(grad_branch, out_full).astype(BF16)
    sent = exchange_group(
        [
            lax.dynamic_slice_in_dim(grad_att_rows, (c ^ absolute(r)) * head_cols, head_cols, 1)
            for r in range(GROUP)
        ]
    )

    def late_beside(given):
        late_branch, late_down = after((grad_branch, grad_down_c), given)
        pieces = exchange_group(
            [
                lax.dynamic_slice_in_dim(late_branch, (c ^ absolute(r)) * head_cols, head_cols, 1)
                for r in range(GROUP)
            ]
        )
        return spread_x(late_down, x), pieces

    grad_att_units, _, _, (down_pair, branch_pieces) = to_units(
        jnp.concatenate(sent, axis=0), 1, late_beside
    )
    mlp_out = lax.psum_scatter(
        mlp_part, ("narrow", "wide"), scatter_dimension=0, tiled=True,
        axis_index_groups=plane_groups(),
    )
    down_four = spread_y(down_pair)
    grad_att = grad_att_units[:, 0].astype(F32)

    unit_logit = jnp.sum(grad_att * (recalled - direct), axis=(1, 2)) * mixing * (1.0 - mixing)
    grad_logit = jnp.sum(
        jnp.where(unit_heads[:, None] == jnp.arange(H)[None], unit_logit[:, None], 0.0), axis=0
    )
    grad_recall = (mix * grad_att).astype(BF16).astype(F32)
    grad_numer = grad_recall / denominator
    grad_denom = -jnp.sum(grad_recall * recalled, axis=-1, keepdims=True) / denominator
    grad_lift_q = (
        jnp.einsum("ute,ude->utd", grad_numer, read_mem, preferred_element_type=F32)
        + grad_denom * read_norm[:, None]
    )
    grad_read_mem = jnp.einsum("utd,ute->ude", lift_q, grad_numer, preferred_element_type=F32)
    grad_read_norm = jnp.sum(grad_denom * lift_q, axis=1)
    grad_read = jnp.concatenate([grad_read_mem, grad_read_norm[:, None]], axis=1)
    grad_direct = after((1.0 - mix) * grad_att, grad_read).astype(BF16)
    dots = attention_back(qkv_units, grad_direct, scale)
    later = jnp.zeros_like(grad_read)
    for k in range(1, segments):
        later = later + lax.ppermute(
            grad_read.astype(BF16), "wide", [(i + k * span, i) for i in range(wide - k * span)]
        )
    later, dots, down_four = lax.optimization_barrier((later / SEG, dots, down_four))
    grad_q_dot, grad_k_dot, grad_v_dot = dots[:, 0], dots[:, 1], dots[:, 2]
    later_mem, later_norm = later[:, :DK], later[:, DK]
    grad_lift_k = (
        jnp.einsum("ute,ude->utd", value_f, later_mem, preferred_element_type=F32)
        + later_norm[:, None]
    )
    grad_v_mem = jnp.einsum("utd,ude->ute", lift_k, later_mem, preferred_element_type=F32)
    grad_units = jnp.stack(
        [
            grad_q_dot + grad_lift_q * elu_slope(query_f),
            grad_k_dot + grad_lift_k * elu_slope(key_f),
            grad_v_dot + grad_v_mem,
        ],
        axis=1,
    ).astype(BF16)
    late = {}

    def spread_late(given):
        late["given"] = given
        parts = after([grad_gate_c, grad_up_c], given)
        return spread_x(jnp.concatenate(parts, axis=1), x)

    grad_projected, _, gate_up_pair = from_units(grad_units, 3, spread_late)
    given = late["given"]
    att_all = join(both_cores(after(att_pieces, given)))
    grad_out_part = t_dot(
        att_all, jnp.concatenate(branch_pieces, axis=0)
    ).astype(BF16)
    grad_out_c = reduce_rows(grad_out_part)
    grad_projected, grad_out_part = lax.optimization_barrier((grad_projected, grad_out_part))
    grad_qkv_part = t_dot(one_all, grad_projected).astype(BF16)
    grad_qkv_c = reduce_rows(grad_qkv_part)
    one_part = dot_t(after(grad_projected, grad_qkv_part), qkv_c).astype(BF16)
    gate_up_y = swap_y(gate_up_pair[0])
    one_part, gate_up_y = lax.optimization_barrier((one_part, gate_up_y))
    one_sums = scatter_start(one_part)
    one_got = scatter_sends(one_sums)
    gate_up_four = gate_up_pair + [gate_up_y, swap_y(after(gate_up_pair[1], gate_up_y))]
    grad_down = assemble(both_cores(after(down_four, one_sums)), c, 1, F32)
    grad_gate_up = assemble(both_cores(after(gate_up_four, one_sums)), c, 2, F32)
    output = (middle + after(mlp_out, one_sums).astype(F32)).astype(BF16)[None]
    one_got, grad_down, grad_gate_up, output = lax.optimization_barrier(
        (one_got, grad_down, grad_gate_up, output)
    )
    grad_normed_one = scatter_total(one_got)
    grad_gain_one = jnp.sum(grad_normed_one * unit_one, axis=0)
    grad_tokens = (
        grad_middle + norm_back(grad_normed_one * gain_one, unit_one, scale_one)
    ).astype(BF16)[None]
    def finish(four, parts):
        return assemble(both_cores(four), c, parts, F32)

    qkv_pair = spread_x(after(grad_qkv_c, grad_normed_one), x)
    qkv_four = spread_y(qkv_pair)
    out_four = spread_y(spread_x(after(grad_out_c, qkv_pair), x))
    grad_out = finish(out_four, 1)
    grad_qkv = finish(qkv_four, 3)

    placed = jnp.zeros((GROUP, DK + 1, DK), BF16)
    placed = lax.dynamic_update_slice_in_dim(placed, after(grad_read, one_sums).astype(BF16), zi * units, 0)
    placed = placed.reshape(2, 4, DK + 1, DK)
    got = []
    for flip in range(4):
        core, y = flip & 1, flip >> 1
        block = placed[:, core * 2 + y]
        if flip:
            block = lax.ppermute(block, "narrow", [(i, i ^ flip) for i in range(4)])
        got.append(block)
    mine = by_index(after(got, grad_normed_one), n)
    if zspan == 2 and segments == 2:
        mine = lax.dynamic_slice_in_dim(mine, zi, 1, 1)
        mine = (mine.astype(F32) + swap_z(mine, 2).astype(F32)).astype(BF16)
        mine = by_bit([mine[:, 0], swap_z(mine, 1)[:, 0]], zi).transpose(1, 0, 2, 3)
    else:
        mine = sum_z(mine)
    heads = by_bit([mine, swap_x(mine)], x).transpose(1, 0, 2, 3, 4)
    heads = heads.reshape(H, DK + 1, DK).astype(F32)

    small = sum_all(jnp.concatenate([grad_gain_one, grad_gain_two, grad_logit]))
    gain_one_sum = lax.dynamic_slice_in_dim(small, w * shard, shard, 0)
    gain_two_sum = lax.dynamic_slice_in_dim(small, D + w * shard, shard, 0)
    return (
        output,
        grad_tokens,
        heads[None, :, :DK],
        heads[None, :, DK],
        grad_qkv,
        grad_out,
        gain_one_sum,
        grad_gate_up,
        grad_down,
        gain_two_sum,
        small[2 * D :],
    )


def solution(mesh):
    return jax.shard_map(
        body,
        mesh=mesh,
        in_specs=(
            P("narrow", "wide", None),
            P("narrow", "wide", None),
            P("wide", None),
            P("wide", None),
            P("wide"),
            P("wide", None),
            P("wide", None),
            P("wide"),
            P(),
            P("narrow", None, None, None),
            P("narrow", None, None),
        ),
        out_specs=(
            P("narrow", "wide", None),
            P("narrow", "wide", None),
            P("narrow", None, None, None),
            P("narrow", None, None),
            P("wide", None),
            P("wide", None),
            P("wide"),
            P("wide", None),
            P("wide", None),
            P("wide"),
            P(),
        ),
        check_vma=False,
    )
```

```python
import functools

import jax
import jax.numpy as jnp
from jax import lax
from jax.experimental import pallas as pl
from jax.experimental.pallas import tpu as pltpu
from jax.sharding import PartitionSpec as P

D = 2048
H = 16
DK = 128
FF = 8192
SEG = 1024
EPSILON = 1e-06
F32 = jnp.float32
BF16 = jnp.bfloat16
GROUP = 8


def swap_x(v):
    n = lax.axis_size("wide")
    return lax.ppermute(v, "wide", [(i, i ^ 1) for i in range(n)])


def swap_y(v):
    return lax.ppermute(v, "narrow", [(i, i ^ 2) for i in range(4)])


def swap_core(v):
    return lax.ppermute(v, "narrow", [(i, i ^ 1) for i in range(4)])


def swap_z(v, d):
    n = lax.axis_size("wide")
    return lax.ppermute(v, "wide", [(i, i ^ (2 * d)) for i in range(n)])


def offset_bits(r):
    return (r >> 1) & 1, (r >> 2) & 1, r & 1


def absolute(r):
    y, core, x = offset_bits(r)
    return y * 4 + core * 2 + x


def send_offset(v, r):
    y, core, x = offset_bits(r)
    n = lax.axis_size("wide")
    flip = y * 2 + core
    route = [(a * n + b, (a ^ flip) * n + (b ^ x)) for a in range(4) for b in range(n)]
    return lax.ppermute(v, ("narrow", "wide"), route)


def plane(v):
    return [v] + [send_offset(v, r) for r in range(1, 4)]


def both_cores(pieces):
    return pieces + [swap_core(p) for p in pieces]


def scatter_start(partial):
    rows = partial.shape[0] // GROUP
    parts = [partial[r * rows : (r + 1) * rows] for r in range(GROUP)]
    sums = [None] * 4
    for r in (3, 1, 2, 0):
        sums[r] = parts[r].astype(F32) + swap_core(parts[4 + r]).astype(F32)
    return [sums[0]] + [v.astype(BF16) for v in sums[1:]]


def scatter_sends(sums):
    return [sums[0]] + [send_offset(sums[r], r) for r in range(1, 4)]


def scatter_total(got):
    return got[0] + got[1].astype(F32) + got[2].astype(F32) + got[3].astype(F32)


def join_kernel(*refs):
    out = refs[-1]
    rows = refs[0].shape[0]
    for i, piece in enumerate(refs[:-1]):
        out[i * rows : (i + 1) * rows] = piece[...]


def join(pieces):
    rows, columns = pieces[0].shape
    step = min(columns, 512)
    return pl.pallas_call(
        join_kernel,
        grid=(columns // step,),
        in_specs=[pl.BlockSpec((rows, step), lambda j: (0, j))] * len(pieces),
        out_specs=pl.BlockSpec((len(pieces) * rows, step), lambda j: (0, j)),
        out_shape=jax.ShapeDtypeStruct((len(pieces) * rows, columns), pieces[0].dtype),
        compiler_params=pltpu.CompilerParams(vmem_limit_bytes=24 * 2**20),
    )(*pieces)


def exchange_group(blocks):
    return lax.optimization_barrier(
        [blocks[0]] + [send_offset(blocks[r], r) for r in range(1, GROUP)]
    )


def by_bit(pair, bit):
    a, b = pair
    return jnp.where(bit == 0, jnp.stack([a, b]), jnp.stack([b, a]))


def by_index(parts, index):
    if len(parts) == 2:
        return by_bit(parts, index)
    out = jnp.zeros((len(parts),) + parts[0].shape, parts[0].dtype)
    for d, part in enumerate(parts):
        out = lax.dynamic_update_slice_in_dim(out, part[None], index ^ d, 0)
    return out


def after(v, *others):
    return lax.optimization_barrier((v, others))[0]


def z_lines():
    n = lax.axis_size("wide")
    return [list(range(x, n, 2)) for x in range(2)]


def eighth_block(parts, x, n):
    c = n * 2 + x

    def columns(eighth):
        return jnp.concatenate(
            [lax.dynamic_slice_in_dim(a, s + eighth * m, m, 1) for a, s, m in parts], axis=1
        )

    give = columns(c ^ 1)
    pair = by_bit([columns(c), swap_x(give)], x)
    return pair.reshape(pair.shape[0] * pair.shape[1], -1), give


def gather_rows(block):
    return lax.all_gather(block, "wide", axis=0, tiled=True, axis_index_groups=z_lines())


def plane_groups():
    n = lax.axis_size("wide")
    return [[a * n + z * 2 + x for a in range(4) for x in range(2)] for z in range(n // 2)]


def reduce_rows(partial):
    return lax.psum_scatter(
        partial, "wide", scatter_dimension=0, tiled=True, axis_index_groups=z_lines()
    )


def gather_gains(v, w):
    n = lax.axis_size("wide")
    blocks = [v]
    for d in range(1, n):
        blocks.append(lax.ppermute(v, "wide", [(i, i ^ d) for i in range(n)]))
    return by_index(blocks, w).transpose(1, 0, 2).reshape(2, -1)


def sum_z(v):
    d = 1
    while d < lax.axis_size("wide") // 2:
        v = (v.astype(F32) + swap_z(v, d).astype(F32)).astype(v.dtype)
        d *= 2
    return v


def sum_all(v):
    v = v + swap_core(v)
    v = v + swap_y(v)
    v = v + swap_x(v)
    return sum_z(v)


def spread_x(summed, x):
    rows = summed.shape[0] // 2
    keep = lax.dynamic_slice_in_dim(summed, x * rows, rows, 0)
    give = lax.dynamic_slice_in_dim(summed, (1 - x) * rows, rows, 0)
    return [keep, swap_x(give)]


def spread_y(pair):
    return pair + [swap_y(p) for p in pair]


def reorder_kernel(order, in_ref, out_ref):
    del order
    out_ref[...] = in_ref[...]


def reorder(rows_by_offset, c):
    rows, columns = rows_by_offset.shape[0] // GROUP, rows_by_offset.shape[1]
    d = c ^ jnp.arange(GROUP, dtype=jnp.int32)
    order = ((d >> 1) & 1) * 4 + ((d >> 2) & 1) * 2 + (d & 1)
    return pl.pallas_call(
        reorder_kernel,
        grid_spec=pltpu.PrefetchScalarGridSpec(
            num_scalar_prefetch=1,
            grid=(GROUP,),
            in_specs=[pl.BlockSpec((rows, columns), lambda i, o: (o[i], 0))],
            out_specs=pl.BlockSpec((rows, columns), lambda i, o: (i, 0)),
        ),
        out_shape=jax.ShapeDtypeStruct(rows_by_offset.shape, rows_by_offset.dtype),
        compiler_params=pltpu.CompilerParams(vmem_limit_bytes=24 * 2**20),
    )(order, rows_by_offset)


def assemble_kernel(width, place, *refs):
    out = refs[GROUP]
    for r in range(GROUP):
        column = pl.multiple_of(place[r] * width, width)
        out[:, pl.ds(column, width)] = refs[r][...].astype(out.dtype)


def assemble(pieces, c, parts, dtype):
    rows = pieces[0].shape[0]
    width = pieces[0].shape[1] // parts
    r = jnp.arange(GROUP, dtype=jnp.int32)
    place = c ^ (((r >> 1) & 1) * 4 + ((r >> 2) & 1) * 2 + (r & 1))
    step = min(rows, (64 * 1024) // width)
    return pl.pallas_call(
        functools.partial(assemble_kernel, width),
        grid_spec=pltpu.PrefetchScalarGridSpec(
            num_scalar_prefetch=1,
            grid=(parts, rows // step),
            in_specs=[pl.BlockSpec((step, width), lambda p, i, o: (i, p))] * GROUP,
            out_specs=pl.BlockSpec((step, GROUP * width), lambda p, i, o: (i, p)),
        ),
        out_shape=jax.ShapeDtypeStruct((rows, parts * GROUP * width), dtype),
        compiler_params=pltpu.CompilerParams(vmem_limit_bytes=24 * 2**20),
    )(place, *pieces)


def assemble_stacked(stacked, c, dtype):
    rows, width = stacked.shape[0] // GROUP, stacked.shape[1]
    r = jnp.arange(GROUP, dtype=jnp.int32)
    place = c ^ (((r >> 1) & 1) * 4 + ((r >> 2) & 1) * 2 + (r & 1))
    return pl.pallas_call(
        functools.partial(assemble_kernel, width),
        grid_spec=pltpu.PrefetchScalarGridSpec(
            num_scalar_prefetch=1,
            grid=(1,),
            in_specs=[
                pl.BlockSpec((rows, width), lambda i, o, r=r: (r, 0)) for r in range(GROUP)
            ],
            out_specs=pl.BlockSpec((rows, GROUP * width), lambda i, o: (0, 0)),
        ),
        out_shape=jax.ShapeDtypeStruct((rows, GROUP * width), dtype),
        compiler_params=pltpu.CompilerParams(vmem_limit_bytes=24 * 2**20),
    )(place, *[stacked] * GROUP)


def pack_kernel(parts, where, in_ref, keep_ref, give_ref):
    for part in range(parts):
        keep = pl.multiple_of(part * 2 * DK + where[1] * DK, DK)
        give = pl.multiple_of(part * 2 * DK + (1 - where[1]) * DK, DK)
        keep_ref[0, part] = in_ref[:, pl.ds(keep, DK)]
        give_ref[0, part] = in_ref[:, pl.ds(give, DK)]


def pack(flat, x, zi):
    step = flat.shape[0] // GROUP
    parts = flat.shape[1] // (2 * DK)
    block = pl.BlockSpec((1, parts, step, DK), lambda u, d, w: (u, 0, w[0] ^ d, 0))
    shape = jax.ShapeDtypeStruct((4, parts, 2 * step, DK), flat.dtype)
    return pl.pallas_call(
        functools.partial(pack_kernel, parts),
        grid_spec=pltpu.PrefetchScalarGridSpec(
            num_scalar_prefetch=1,
            grid=(4, 2),
            in_specs=[pl.BlockSpec((step, parts * 2 * DK), lambda u, d, w: (u * 2 + d, 0))],
            out_specs=[block, block],
        ),
        out_shape=[shape, shape],
        compiler_params=pltpu.CompilerParams(vmem_limit_bytes=24 * 2**20),
    )(jnp.stack([x, zi]).astype(jnp.int32), flat)


def unpack_kernel(parts, where, own_ref, other_ref, out_ref):
    for part in range(parts):
        own = pl.multiple_of(part * 2 * DK + where[1] * DK, DK)
        other = pl.multiple_of(part * 2 * DK + (1 - where[1]) * DK, DK)
        out_ref[:, pl.ds(own, DK)] = own_ref[0, part]
        out_ref[:, pl.ds(other, DK)] = other_ref[0, part]


def unpack(own, other, x, zi):
    units, parts, rows = own.shape[:3]
    step = rows // 2
    block = pl.BlockSpec((1, parts, step, DK), lambda u, d, w: (u, 0, w[0] ^ d, 0))
    return pl.pallas_call(
        functools.partial(unpack_kernel, parts),
        grid_spec=pltpu.PrefetchScalarGridSpec(
            num_scalar_prefetch=1,
            grid=(units, 2),
            in_specs=[block, block],
            out_specs=pl.BlockSpec((step, parts * 2 * DK), lambda u, d, w: (u * 2 + d, 0)),
        ),
        out_shape=jax.ShapeDtypeStruct((units * rows, parts * 2 * DK), own.dtype),
        compiler_params=pltpu.CompilerParams(vmem_limit_bytes=24 * 2**20),
    )(jnp.stack([x, zi]).astype(jnp.int32), own, other)


ROWS = 256


def masked_probs(queries, keys, first, scale):
    scores = lax.dot_general(
        queries, keys, (((1,), (1,)), ((), ())), preferred_element_type=F32
    ) * scale
    row = lax.broadcasted_iota(jnp.int32, scores.shape, 0) + first
    col = lax.broadcasted_iota(jnp.int32, scores.shape, 1)
    scores = jnp.where(col <= row, scores, -1e30)
    raised = jnp.exp(scores - jnp.max(scores, axis=-1, keepdims=True))
    return raised / jnp.sum(raised, axis=-1, keepdims=True)


def attention_kernel(scale, qkv_ref, out_ref):
    for first in range(0, SEG, ROWS):
        end = first + ROWS
        probs = masked_probs(qkv_ref[0, 0, first:end], qkv_ref[0, 1, :end], first, scale)
        out_ref[0, first:end] = jnp.dot(
            probs.astype(BF16), qkv_ref[0, 2, :end], preferred_element_type=F32
        )


def attention(qkv, scale):
    units = qkv.shape[0]
    return pl.pallas_call(
        functools.partial(attention_kernel, scale),
        grid=(units,),
        in_specs=[pl.BlockSpec((1, 3, SEG, DK), lambda u: (u, 0, 0, 0))],
        out_specs=pl.BlockSpec((1, SEG, DK), lambda u: (u, 0, 0)),
        out_shape=jax.ShapeDtypeStruct((units, SEG, DK), F32),
        compiler_params=pltpu.CompilerParams(vmem_limit_bytes=40 * 2**20),
        cost_estimate=pl.CostEstimate(
            flops=units * 4 * SEG * SEG * DK, bytes_accessed=units * SEG * DK * 10,
            transcendentals=units * SEG * SEG,
        ),
    )(qkv)


def attention_back_kernel(scale, qkv_ref, grad_ref, out_ref):
    out_ref[0, 1] = jnp.zeros((SEG, DK), F32)
    out_ref[0, 2] = jnp.zeros((SEG, DK), F32)
    for first in range(0, SEG, ROWS):
        end = first + ROWS
        queries, keys, values = qkv_ref[0, 0, first:end], qkv_ref[0, 1, :end], qkv_ref[0, 2, :end]
        grad = grad_ref[0, first:end]
        probs = masked_probs(queries, keys, first, scale)
        grad_probs = lax.dot_general(
            grad, values, (((1,), (1,)), ((), ())), preferred_element_type=F32
        )
        inner = jnp.sum(probs * grad_probs, axis=-1, keepdims=True)
        grad_scores = (probs * (grad_probs - inner)).astype(BF16)
        out_ref[0, 0, first:end] = jnp.dot(
            grad_scores, keys, preferred_element_type=F32
        ) * scale
        out_ref[0, 1, :end] += lax.dot_general(
            grad_scores, queries, (((0,), (0,)), ((), ())), preferred_element_type=F32
        )
        out_ref[0, 2, :end] += lax.dot_general(
            probs.astype(BF16), grad, (((0,), (0,)), ((), ())), preferred_element_type=F32
        )
    out_ref[0, 1] = out_ref[0, 1] * scale


def attention_back(qkv, grad, scale):
    units = qkv.shape[0]
    return pl.pallas_call(
        functools.partial(attention_back_kernel, scale),
        grid=(units,),
        in_specs=[
            pl.BlockSpec((1, 3, SEG, DK), lambda u: (u, 0, 0, 0)),
            pl.BlockSpec((1, SEG, DK), lambda u: (u, 0, 0)),
        ],
        out_specs=pl.BlockSpec((1, 3, SEG, DK), lambda u: (u, 0, 0, 0)),
        out_shape=jax.ShapeDtypeStruct((units, 3, SEG, DK), F32),
        compiler_params=pltpu.CompilerParams(vmem_limit_bytes=48 * 2**20),
        cost_estimate=pl.CostEstimate(
            flops=units * 10 * SEG * SEG * DK, bytes_accessed=units * SEG * DK * 20,
            transcendentals=units * SEG * SEG,
        ),
    )(qkv, grad)


def dot(a, b):
    return jnp.dot(a, b, preferred_element_type=F32)


def dot_t(a, b):
    return lax.dot_general(a, b, (((1,), (1,)), ((), ())), preferred_element_type=F32)


def t_dot(a, b):
    return lax.dot_general(a, b, (((0,), (0,)), ((), ())), preferred_element_type=F32)


def norm_back(grad_unit, unit_rows, scale_rows):
    return scale_rows * (
        grad_unit - unit_rows * jnp.mean(grad_unit * unit_rows, axis=-1, keepdims=True)
    )


def elu_slope(inputs):
    return jnp.where(inputs > 0, 1.0, jnp.exp(jnp.minimum(inputs, 0.0)))


def body(
    tokens,
    cotangent,
    qkv_weight,
    out_weight,
    gain_attn,
    gate_up_weight,
    down_weight,
    gain_mlp,
    gate_logit,
    memory_in,
    normalizer_in,
):
    wide = lax.axis_size("wide")
    n = lax.axis_index("narrow")
    w = lax.axis_index("wide")
    z, x = w // 2, w % 2
    c = n * 2 + x
    rows_here = tokens.shape[1]
    shard = qkv_weight.shape[0]
    span = SEG // rows_here
    zspan = span // 2
    zi = z % zspan
    segments = wide // span
    units = GROUP // zspan
    head_cols = D // GROUP
    ff_cols = FF // GROUP
    scale = DK ** (-0.5)

    first, _ = eighth_block(
        [(qkv_weight, 0, head_cols), (qkv_weight, D, head_cols), (qkv_weight, 2 * D, head_cols),
         (out_weight, 0, head_cols)], x, n
    )
    first_c = gather_rows(first)
    qkv_c = first_c[:, : 3 * head_cols]

    inputs = tokens[0].astype(F32)
    scale_one = lax.rsqrt(jnp.mean(inputs * inputs, axis=-1, keepdims=True) + EPSILON)
    unit_one = inputs * scale_one
    gains = gather_gains(jnp.stack([gain_attn, gain_mlp]), w).astype(F32)
    gain_one, gain_two = gains[0], gains[1]
    normed_one = (unit_one * gain_one).astype(BF16)
    one_pieces = plane(after(normed_one, first))

    cot = cotangent[0]

    def to_units(flat, parts, beside=()):
        if zspan == 2:
            keep, given = pack(flat, x, zi)
            blocks = [keep, swap_z(given, 1)]
        else:
            v = flat.reshape(2, 2, 2, rows_here, parts, 2, DK).transpose(2, 5, 0, 1, 4, 3, 6)
            v = by_bit([v[0], v[1]], x)
            v = v.transpose(1, 2, 3, 4, 0, 5, 6).reshape(GROUP, parts, 2 * rows_here, DK)
            blocks = []
            for d in range(zspan):
                block = lax.dynamic_slice_in_dim(v, (zi ^ d) * units, units, 0)
                given = block
                blocks.append(block if d == 0 else swap_z(block, d))
        if callable(beside):
            beside = beside(given)
        blocks, beside = lax.optimization_barrier((blocks, beside))
        v = by_index(blocks, zi)
        return v.transpose(1, 2, 0, 3, 4).reshape(units, parts, SEG, DK), given, blocks[-1], beside

    def from_units(v, parts, beside=()):
        v = v.reshape(units, parts, zspan, 2 * rows_here, DK)
        blocks = []
        for d in range(zspan):
            block = lax.dynamic_slice_in_dim(v, zi ^ d, 1, 2)[:, :, 0]
            given = block
            blocks.append(block if d == 0 else swap_z(block, d))
        if callable(beside):
            beside = beside(given)
        blocks, beside = lax.optimization_barrier((blocks, beside))
        if zspan == 2:
            return unpack(blocks[0], blocks[1], x, zi), blocks[-1], beside
        v = by_index(blocks, zi).reshape(2, 2, 2, parts, 2, rows_here, DK)
        v = by_bit([v[:, :, :, :, 0], v[:, :, :, :, 1]], x)
        v = v.transpose(2, 3, 0, 5, 4, 1, 6)
        return v.reshape(GROUP * rows_here, parts * head_cols), blocks[-1], beside

    one_all = join(both_cores(one_pieces))
    projected = dot(one_all, qkv_c).astype(BF16)

    def late_blocks(given):
        late_weight = after(gate_up_weight, given)
        return [eighth_block([(late_weight, s, ff_cols)], x, n)[0] for s in (0, FF)]

    qkv_units, given, swapped, (gate_block, up_block) = to_units(
        projected, 3, late_blocks
    )
    gate_c = gather_rows(after(gate_block, swapped))
    up_c = gather_rows(after(up_block, swapped))
    queries, keys, values = qkv_units[:, 0], qkv_units[:, 1], qkv_units[:, 2]

    head_count = max(1, units // 4)
    seq_count = units // head_count
    first_head = (zi * units) // 4
    first_seq = (zi * units) % 4
    held = jnp.concatenate([memory_in[0], normalizer_in[0][:, None]], axis=1)
    fetched = []
    for offset in range(4):
        core, y = offset >> 1, offset & 1
        flip = y * 2 + core
        block = lax.dynamic_slice_in_dim(
            held, ((n ^ flip) * 2 + x) * 2 + first_head, head_count, 0
        )
        if flip:
            block = lax.ppermute(block, "narrow", [(i, i ^ flip) for i in range(4)])
        fetched.append(block)
    mem_in = jnp.stack(fetched, axis=1)
    mem_in = lax.dynamic_slice_in_dim(mem_in, first_seq, seq_count, 1)
    mem_in = mem_in.reshape(units, DK + 1, DK)

    query_f, key_f, value_f = (a.astype(F32) for a in (queries, keys, values))
    lift_q = jax.nn.elu(query_f) + 1.0
    lift_k = jax.nn.elu(key_f) + 1.0
    part_mem = jnp.einsum("utd,ute->ude", lift_k, value_f, preferred_element_type=F32)
    part_norm = jnp.sum(lift_k, axis=1)
    part = jnp.concatenate([part_mem, part_norm[:, None]], axis=1) / SEG
    direct = attention(after(qkv_units, part), scale)
    read = mem_in
    for k in range(1, segments):
        read = read + lax.ppermute(
            part, "wide", [(i, i + k * span) for i in range(wide - k * span)]
        )
    read_mem, read_norm = read[:, :DK], read[:, DK]
    numerator = jnp.einsum("utd,ude->ute", lift_q, read_mem, preferred_element_type=F32)
    denominator = jnp.sum(lift_q * read_norm[:, None], axis=-1, keepdims=True)
    recalled = numerator / denominator

    unit_heads = c * 2 + (zi * units + jnp.arange(units)) // 4
    mixing = jax.nn.sigmoid(gate_logit[unit_heads])
    mix = mixing[:, None, None]
    attended_units = (mix * recalled + (1.0 - mix) * direct).astype(BF16)

    def late_out(given):
        out_late, down_late = after((first_c[:, 3 * head_cols :], down_weight), given)
        return plane(out_late), eighth_block([(down_late, 0, ff_cols)], x, n)[0]

    attended_c, swapped, (out_pieces, down_block) = from_units(
        attended_units[:, None], 1, late_out
    )
    down_c = gather_rows(down_block)
    attended_c = attended_c.reshape(GROUP, rows_here, head_cols)
    sent = exchange_group([attended_c[r] for r in range(GROUP)])
    out_full = assemble(both_cores(out_pieces), c, 1, BF16)
    attended = assemble_stacked(jnp.concatenate(sent, axis=0), c, BF16)

    middle = inputs + dot(attended, out_full)
    scale_two = lax.rsqrt(jnp.mean(middle * middle, axis=-1, keepdims=True) + EPSILON)
    unit_two = middle * scale_two
    normed_two = (unit_two * gain_two).astype(BF16)
    two_pieces = plane(normed_two)
    cot_pieces = plane(after(cot, two_pieces))
    two_all = join(both_cores(two_pieces))
    gate_short = dot(two_all, gate_c).astype(BF16)
    up_short = dot(after(two_all, gate_short), up_c).astype(BF16)
    cot_pieces, up_short = lax.optimization_barrier((cot_pieces, up_short))
    gate_part, up_part = gate_short.astype(F32), up_short.astype(F32)
    gate_sig = jax.nn.sigmoid(gate_part)
    activation = (gate_part * gate_sig * up_part).astype(BF16)
    cot_all = join(both_cores(cot_pieces))
    grad_down_part = t_dot(cot_all, activation).astype(BF16)
    grad_down_c = reduce_rows(grad_down_part)
    att_pieces = plane(after(attended, cot_all))
    grad_activ = dot(after(cot_all, grad_down_part), down_c)
    grad_gate = (
        grad_activ * up_part * gate_sig * (1.0 + gate_part * (1.0 - gate_sig))
    ).astype(BF16)
    grad_upper = (grad_activ * gate_part * gate_sig).astype(BF16)
    back = (dot_t(grad_gate, gate_c) + dot_t(grad_upper, up_c)).astype(BF16)
    back, att_pieces = lax.optimization_barrier((back, att_pieces))
    grad_gate_part = t_dot(two_all, after(grad_gate, back)).astype(BF16)
    back_sums, grad_gate_part = lax.optimization_barrier((scatter_start(back), grad_gate_part))
    back_got = scatter_sends(back_sums)
    grad_gate_c = reduce_rows(grad_gate_part)
    grad_up_part = t_dot(two_all, after(grad_upper, grad_gate_part)).astype(BF16)
    grad_up_c = reduce_rows(grad_up_part)
    mlp_part = reorder(dot_t(after(activation, grad_up_part), down_c).astype(BF16), c)
    back_got, mlp_part, grad_down_c = lax.optimization_barrier(
        (back_got, mlp_part, grad_down_c)
    )
    grad_normed_two = scatter_total(back_got)
    grad_gain_two = jnp.sum(grad_normed_two * unit_two, axis=0)
    grad_middle = cot.astype(F32) + norm_back(grad_normed_two * gain_two, unit_two, scale_two)

    grad_branch = grad_middle.astype(BF16)
    grad_att_rows = dot_t(grad_branch, out_full).astype(BF16)
    sent = exchange_group(
        [
            lax.dynamic_slice_in_dim(grad_att_rows, (c ^ absolute(r)) * head_cols, head_cols, 1)
            for r in range(GROUP)
        ]
    )

    def late_beside(given):
        late_branch, late_down = after((grad_branch, grad_down_c), given)
        pieces = exchange_group(
            [
                lax.dynamic_slice_in_dim(late_branch, (c ^ absolute(r)) * head_cols, head_cols, 1)
                for r in range(GROUP)
            ]
        )
        return spread_x(late_down, x), pieces

    grad_att_units, _, _, (down_pair, branch_pieces) = to_units(
        jnp.concatenate(sent, axis=0), 1, late_beside
    )
    mlp_out = lax.psum_scatter(
        mlp_part, ("narrow", "wide"), scatter_dimension=0, tiled=True,
        axis_index_groups=plane_groups(),
    )
    down_four = spread_y(down_pair)
    grad_att = grad_att_units[:, 0].astype(F32)

    unit_logit = jnp.sum(grad_att * (recalled - direct), axis=(1, 2)) * mixing * (1.0 - mixing)
    grad_logit = jnp.sum(
        jnp.where(unit_heads[:, None] == jnp.arange(H)[None], unit_logit[:, None], 0.0), axis=0
    )
    grad_recall = (mix * grad_att).astype(BF16).astype(F32)
    grad_numer = grad_recall / denominator
    grad_denom = -jnp.sum(grad_recall * recalled, axis=-1, keepdims=True) / denominator
    grad_lift_q = (
        jnp.einsum("ute,ude->utd", grad_numer, read_mem, preferred_element_type=F32)
        + grad_denom * read_norm[:, None]
    )
    grad_read_mem = jnp.einsum("utd,ute->ude", lift_q, grad_numer, preferred_element_type=F32)
    grad_read_norm = jnp.sum(grad_denom * lift_q, axis=1)
    grad_read = jnp.concatenate([grad_read_mem, grad_read_norm[:, None]], axis=1)
    grad_direct = after((1.0 - mix) * grad_att, grad_read).astype(BF16)
    dots = attention_back(qkv_units, grad_direct, scale)
    later = jnp.zeros_like(grad_read)
    for k in range(1, segments):
        later = later + lax.ppermute(
            grad_read.astype(BF16), "wide", [(i + k * span, i) for i in range(wide - k * span)]
        )
    later, dots, down_four = lax.optimization_barrier((later / SEG, dots, down_four))
    grad_q_dot, grad_k_dot, grad_v_dot = dots[:, 0], dots[:, 1], dots[:, 2]
    later_mem, later_norm = later[:, :DK], later[:, DK]
    grad_lift_k = (
        jnp.einsum("ute,ude->utd", value_f, later_mem, preferred_element_type=F32)
        + later_norm[:, None]
    )
    grad_v_mem = jnp.einsum("utd,ude->ute", lift_k, later_mem, preferred_element_type=F32)
    grad_units = jnp.stack(
        [
            grad_q_dot + grad_lift_q * elu_slope(query_f),
            grad_k_dot + grad_lift_k * elu_slope(key_f),
            grad_v_dot + grad_v_mem,
        ],
        axis=1,
    ).astype(BF16)
    late = {}

    def spread_late(given):
        late["given"] = given
        parts = after([grad_gate_c, grad_up_c], given)
        pair = spread_x(jnp.concatenate(parts, axis=1), x)
        return pair, swap_y(pair[0])

    grad_projected, _, (gate_up_pair, gate_up_y) = from_units(grad_units, 3, spread_late)
    given = late["given"]
    att_all = join(both_cores(after(att_pieces, given)))
    grad_out_part = t_dot(
        att_all, jnp.concatenate(branch_pieces, axis=0)
    ).astype(BF16)
    grad_out_c = reduce_rows(grad_out_part)
    grad_projected, grad_out_part = lax.optimization_barrier((grad_projected, grad_out_part))
    grad_qkv_part = t_dot(one_all, grad_projected).astype(BF16)
    grad_qkv_c = reduce_rows(grad_qkv_part)
    one_part = dot_t(after(grad_projected, grad_qkv_part), qkv_c).astype(BF16)
    gate_up_last = swap_y(gate_up_pair[1])
    one_part, gate_up_last = lax.optimization_barrier((one_part, gate_up_last))
    one_sums = scatter_start(one_part)
    one_got = scatter_sends(one_sums)
    gate_up_four = gate_up_pair + [gate_up_y, gate_up_last]
    grad_down = assemble(both_cores(after(down_four, one_sums)), c, 1, F32)
    grad_gate_up = assemble(both_cores(after(gate_up_four, one_sums)), c, 2, F32)
    output = (middle + after(mlp_out, one_sums).astype(F32)).astype(BF16)[None]
    one_got, grad_down, grad_gate_up, output = lax.optimization_barrier(
        (one_got, grad_down, grad_gate_up, output)
    )
    grad_normed_one = scatter_total(one_got)
    grad_gain_one = jnp.sum(grad_normed_one * unit_one, axis=0)
    grad_tokens = (
        grad_middle + norm_back(grad_normed_one * gain_one, unit_one, scale_one)
    ).astype(BF16)[None]
    def finish(four, parts):
        return assemble(both_cores(four), c, parts, F32)

    qkv_pair = spread_x(after(grad_qkv_c, grad_normed_one), x)
    qkv_four = spread_y(qkv_pair)
    out_four = spread_y(spread_x(after(grad_out_c, qkv_pair), x))
    grad_out = finish(out_four, 1)
    grad_qkv = finish(qkv_four, 3)

    placed = jnp.zeros((GROUP, DK + 1, DK), BF16)
    placed = lax.dynamic_update_slice_in_dim(placed, after(grad_read, one_sums).astype(BF16), zi * units, 0)
    placed = placed.reshape(2, 4, DK + 1, DK)
    got = []
    for flip in range(4):
        core, y = flip & 1, flip >> 1
        block = placed[:, core * 2 + y]
        if flip:
            block = lax.ppermute(block, "narrow", [(i, i ^ flip) for i in range(4)])
        got.append(block)
    mine = by_index(after(got, grad_normed_one), n)
    if zspan == 2 and segments == 2:
        mine = lax.dynamic_slice_in_dim(mine, zi, 1, 1)
        mine = (mine.astype(F32) + swap_z(mine, 2).astype(F32)).astype(BF16)
        mine = by_bit([mine[:, 0], swap_z(mine, 1)[:, 0]], zi).transpose(1, 0, 2, 3)
    else:
        mine = sum_z(mine)
    heads = by_bit([mine, swap_x(mine)], x).transpose(1, 0, 2, 3, 4)
    heads = heads.reshape(H, DK + 1, DK).astype(F32)

    small = sum_all(jnp.concatenate([grad_gain_one, grad_gain_two, grad_logit]))
    gain_one_sum = lax.dynamic_slice_in_dim(small, w * shard, shard, 0)
    gain_two_sum = lax.dynamic_slice_in_dim(small, D + w * shard, shard, 0)
    return (
        output,
        grad_tokens,
        heads[None, :, :DK],
        heads[None, :, DK],
        grad_qkv,
        grad_out,
        gain_one_sum,
        grad_gate_up,
        grad_down,
        gain_two_sum,
        small[2 * D :],
    )


def solution(mesh):
    return jax.shard_map(
        body,
        mesh=mesh,
        in_specs=(
            P("narrow", "wide", None),
            P("narrow", "wide", None),
            P("wide", None),
            P("wide", None),
            P("wide"),
            P("wide", None),
            P("wide", None),
            P("wide"),
            P(),
            P("narrow", None, None, None),
            P("narrow", None, None),
        ),
        out_specs=(
            P("narrow", "wide", None),
            P("narrow", "wide", None),
            P("narrow", None, None, None),
            P("narrow", None, None),
            P("wide", None),
            P("wide", None),
            P("wide"),
            P("wide", None),
            P("wide", None),
            P("wide"),
            P(),
        ),
        check_vma=False,
    )
```
